32 devices in a mesh: groups: 2 (over y), tensor: 8 (over z, x), dp: 2 (over core).
Axes of the slice: x: 2, y: 2, z: 4, core: 2. Of those that a mesh axis runs over, the one named last changes fastest.
Arguments:
- features: bfloat16 [4096, 1024], P('tensor', ('groups', 'dp')), parts along dimension 1, may hold values from -6 to 6
- table_up: int32 [4, 64], replicated, may hold values from 0 to 1
- table_down: int32 [4, 64], replicated, may hold values from 0 to 1
- w_up: bfloat16 [4, 256, 16384], P(None, None, 'tensor'), may hold values from -0.1875 to 0.1875
- u_up: bfloat16 [4096, 256], P('tensor'), may hold values from -0.09375 to 0.09375
- v_up: bfloat16 [16384, 256], P('tensor'), may hold values from -0.375 to 0.375
- w_down: bfloat16 [4, 256, 16384], P(None, None, 'tensor'), may hold values from -0.09375 to 0.09375
- u_down: bfloat16 [4096, 256], P('tensor'), may hold values from -0.375 to 0.375
- v_down: bfloat16 [16384, 256], P('tensor'), may hold values from -0.046875 to 0.046875
- cotangent: bfloat16 [4096, 1024], P('tensor', ('groups', 'dp')), parts along dimension 1, may hold values from -6 to 6
Outputs:
- output: bfloat16 [4096, 1024], P('tensor', ('groups', 'dp')), parts along dimension 1
- grad_features: bfloat16 [4096, 1024], P('tensor', ('groups', 'dp')), parts along dimension 1
- grad_w_up: float32 [8, 256, 16384], P('groups', 'dp', 'tensor'), parts along dimension 0
- grad_w_down: float32 [8, 256, 16384], P('groups', 'dp', 'tensor'), parts along dimension 0
- grad_u_up: float32 [8192, 256], P(('groups', 'tensor'), 'dp'), parts along dimension 0
- grad_v_up: float32 [32768, 256], P(('groups', 'tensor'), 'dp'), parts along dimension 0
- grad_u_down: float32 [8192, 256], P(('groups', 'tensor'), 'dp'), parts along dimension 0
- grad_v_down: float32 [32768, 256], P(('groups', 'tensor'), 'dp'), parts along dimension 0
The draws below stay inside these ranges and needn't reach their ends.
There are 2 independent parts, one for each index of `groups`. The reference program is written for one: setup_inputs(seed, part) draws one part's arguments, and reference() takes and returns one part's arrays. A program takes and returns all parts, laid end to end along the dimension named above; an argument that names none is the same for every part. Nothing has to cross between parts.
Inputs may be any that keep to these rules, and one draw needn't show every extreme that they name: `table_up`: each entry names one block of 256 features within a panel of 512 features. `table_down`: each entry names one block of 256 features within a panel of 512 features.
All inputs are finite; a program needn't handle non-finite values.
Results may differ from the reference program's by a relative error of at most 0.006.
Values may be sent and summed in bfloat16 or wider, within the bound.
A program may use at most 192 MiB of HBM per device.

```python
import math
import jax
import jax.numpy as jnp
from jax import lax

D = 4096
FF = 16384
BLOCK = 256
RANK = 256
SLOTS = 4
PANELS = 8
TOKENS = 512


def with_ends(values, rng, least, high):
    longest = values.shape.index(max(values.shape))
    spots = []
    for shift in (0, 1):
        where = [jax.random.randint(jax.random.fold_in(rng, axis), (), 0, length) for axis, length in enumerate(values.shape)]
        where[longest] = (where[longest] + shift) % values.shape[longest]
        spots.append(tuple(where))
    return values.at[spots[0]].set(least).at[spots[1]].set(high)


def block_scale(key, dims, cuts, smallest, high):
    level = 1.0
    for axis_at, parts in cuts:
        draws = jax.random.uniform(jax.random.fold_in(jax.random.fold_in(key, 6), axis_at), (parts,), jnp.float32, smallest / len(cuts), high / len(cuts))
        level = level * jnp.repeat(jnp.exp(draws), dims[axis_at] // parts).reshape((-1,) + (1,) * (len(dims) - 1 - axis_at))
    return level


def bell_draw(key, extent, scale, most, shards=(), kind=jnp.bfloat16):
    result = scale * jax.random.normal(key, extent, jnp.float32)
    if shards:
        result = result * block_scale(key, extent, shards, -0.22, 0.18)
    return jnp.clip(result, -most, most).astype(kind)


def setup_inputs(seed: int = 0, part: int = 0) -> dict:
    key_of = jax.random.split(jax.random.key(seed), 11)
    part_splits = jax.random.split(jax.random.fold_in(key_of[10], part), 11)
    return {
        "features": bell_draw(part_splits[0], (D, TOKENS), 1.0, 6.0, ((0, 8), (1, 2))),
        "table_up": with_ends(jax.random.randint(key_of[1], (SLOTS, FF // BLOCK), 0, D // (PANELS * BLOCK)), jax.random.fold_in(key_of[1], 1), 0, (D // (PANELS * BLOCK)) - 1).astype(jnp.int32),
        "table_down": with_ends(jax.random.randint(key_of[2], (SLOTS, FF // BLOCK), 0, D // (PANELS * BLOCK)), jax.random.fold_in(key_of[2], 1), 0, (D // (PANELS * BLOCK)) - 1).astype(jnp.int32),
        "w_up": bell_draw(key_of[3], (SLOTS, BLOCK, FF), (SLOTS * BLOCK) ** -0.5, 0.1875, ((2, 8),)),
        "u_up": bell_draw(key_of[4], (D, RANK), D ** -0.5, 0.09375, ((0, 8),)),
        "v_up": bell_draw(key_of[5], (FF, RANK), RANK ** -0.5, 0.375, ((0, 8),)),
        "w_down": bell_draw(key_of[6], (SLOTS, BLOCK, FF), (SLOTS * FF * BLOCK // D) ** -0.5, 0.09375, ((2, 8),)),
        "u_down": bell_draw(key_of[7], (D, RANK), RANK ** -0.5, 0.375, ((0, 8),)),
        "v_down": bell_draw(key_of[8], (FF, RANK), FF ** -0.5, 0.046875, ((0, 8),)),
        "cotangent": bell_draw(part_splits[9], (D, TOKENS), 1.0, 6.0, ((0, 8), (1, 2))),
    }


root_half = 1.0 / math.sqrt(2.0)
inv_root_tau = 1.0 / math.sqrt(2.0 * math.pi)

def gelu_value(values):
    return 0.5 * values * (1.0 + lax.erf(values * root_half))

def gelu_slope(values):
    return 0.5 * (1.0 + lax.erf(values * root_half)) + values * jnp.exp(-0.5 * values * values) * inv_root_tau

def source_blocks(selector, slot_index):
    hidden_blocks = FF // BLOCK
    per_panel = D // (PANELS * BLOCK)
    block_ids = jnp.arange(hidden_blocks, dtype=jnp.int32)
    panel_ids = block_ids // (hidden_blocks // PANELS)
    if slot_index > 0:
        panel_ids = jnp.bitwise_xor(panel_ids, jnp.int32(1 << slot_index - 1))
    return (panel_ids * per_panel + selector[slot_index]).astype(jnp.int32)

def select_rows(matrix, sources):
    return jnp.take(matrix.reshape(D // BLOCK, BLOCK, TOKENS), sources, axis=0)

def gather_product(weights, matrix, selector):
    summed = jnp.zeros((FF // BLOCK, BLOCK, TOKENS), jnp.float32)
    for slot_index in range(SLOTS):
        picked = select_rows(matrix, source_blocks(selector, slot_index)).astype(jnp.float32)
        blocks = weights[slot_index].reshape(BLOCK, FF // BLOCK, BLOCK).astype(jnp.float32)
        summed = summed + jnp.einsum('rcw,crt->cwt', blocks, picked)
    return summed.reshape(FF, TOKENS)

def scatter_product(weights, hidden_values, selector):
    spread = hidden_values.reshape(FF // BLOCK, BLOCK, TOKENS).astype(jnp.float32)
    summed = jnp.zeros((D // BLOCK, BLOCK, TOKENS), jnp.float32)
    for slot_index in range(SLOTS):
        blocks = weights[slot_index].reshape(BLOCK, FF // BLOCK, BLOCK).astype(jnp.float32)
        summed = summed.at[source_blocks(selector, slot_index)].add(jnp.einsum('rcw,cwt->crt', blocks, spread))
    return summed.reshape(D, TOKENS)

def weight_grad(matrix, hidden_values, selector):
    spread = hidden_values.reshape(FF // BLOCK, BLOCK, TOKENS).astype(jnp.float32)
    grads = []
    for slot_index in range(SLOTS):
        picked = select_rows(matrix, source_blocks(selector, slot_index)).astype(jnp.float32)
        grads.append(jnp.einsum('crt,cwt->rcw', picked, spread).reshape(BLOCK, FF))
    return jnp.stack(grads)

def reference(features, table_up, table_down, w_up, u_up, v_up, w_down, u_down, v_down, cotangent):
    a_up = jnp.dot(u_up.T, features, preferred_element_type=jnp.float32)
    a_up_b = a_up.astype(jnp.bfloat16)
    preact = gather_product(w_up, features, table_up) + jnp.dot(v_up, a_up_b, preferred_element_type=jnp.float32)
    activation = gelu_value(preact).astype(jnp.bfloat16)
    a_down = jnp.dot(v_down.T, activation, preferred_element_type=jnp.float32)
    a_down_b = a_down.astype(jnp.bfloat16)
    output = (scatter_product(w_down, activation, table_down) + jnp.dot(u_down, a_down_b, preferred_element_type=jnp.float32)).astype(jnp.bfloat16)
    b_down = jnp.dot(u_down.T, cotangent, preferred_element_type=jnp.float32)
    b_down_b = b_down.astype(jnp.bfloat16)
    grad_act = gather_product(w_down, cotangent, table_down) + jnp.dot(v_down, b_down_b, preferred_element_type=jnp.float32)
    grad_pre = (grad_act * gelu_slope(preact)).astype(jnp.bfloat16)
    b_up = jnp.dot(v_up.T, grad_pre, preferred_element_type=jnp.float32)
    b_up_b = b_up.astype(jnp.bfloat16)
    grad_features = (scatter_product(w_up, grad_pre, table_up) + jnp.dot(u_up, b_up_b, preferred_element_type=jnp.float32)).astype(jnp.bfloat16)
    grad_w_up = weight_grad(features, grad_pre, table_up)
    grad_w_down = weight_grad(cotangent, activation, table_down)
    grad_u_up = jnp.dot(features, b_up_b.T, preferred_element_type=jnp.float32)
    grad_v_up = jnp.dot(grad_pre, a_up_b.T, preferred_element_type=jnp.float32)
    grad_u_down = jnp.dot(cotangent, a_down_b.T, preferred_element_type=jnp.float32)
    grad_v_down = jnp.dot(activation, b_down_b.T, preferred_element_type=jnp.float32)
    return (output, grad_features, grad_w_up, grad_w_down, grad_u_up, grad_v_up, grad_u_down, grad_v_down)
```

```python
import functools
import math

import jax
import jax.numpy as jnp
from jax import lax
from jax.experimental import pallas as pl
from jax.experimental.pallas import tpu as pltpu
from jax.sharding import PartitionSpec as P

root_half = 1.0 / math.sqrt(2.0)
inv_root_tau = 1.0 / math.sqrt(2.0 * math.pi)


def from_partner(array, axis, distance):
    return lax.ppermute(array, axis, [(i, i ^ 1 << distance) for i in range(lax.axis_size(axis))])


def gelu_value(values):
    return 0.5 * values * (1.0 + lax.erf(values * root_half))


def gelu_slope(values):
    return (
        0.5 * (1.0 + lax.erf(values * root_half))
        + values * jnp.exp(-0.5 * values * values) * inv_root_tau
    )


def panel_trade(values, bit_index):
    return from_partner(values, "tensor", bit_index)


def partial_trade(values, bit_index):
    return from_partner(values, "tensor", bit_index)


def block_ids(device, geometry):
    block_rows, hidden, column_width, block_count = (
        geometry[3],
        geometry[4],
        geometry[5],
        geometry[6],
    )
    starts = device * hidden + jnp.arange(block_count, dtype=jnp.int32) * column_width
    return starts // block_rows


def lookup(selector, slot_index, device, geometry):
    return jnp.take(selector[slot_index], block_ids(device, geometry), axis=0)


def pick_blocks(panel_rows, chosen, block_rows):
    stacked = panel_rows.reshape(panel_rows.shape[0] // block_rows, block_rows, panel_rows.shape[1])
    return jnp.take(stacked, chosen, axis=0)


def place_blocks(portion, chosen, block_rows, panel_size):
    per_panel = panel_size // block_rows
    onehot = (chosen[:, None] == jnp.arange(per_panel, dtype=jnp.int32)[None, :]).astype(
        jnp.float32
    )
    placed = jnp.einsum("bn,brt->nrt", onehot, portion, precision=lax.Precision.HIGHEST)
    return placed.reshape(panel_size, portion.shape[2])


def group_gather(portion, axis_dim, group_bits, device):
    for bit_index in range(group_bits):
        partner_rows = panel_trade(portion, bit_index)
        is_upper = device >> bit_index & 1 == 1
        portion = jnp.where(
            is_upper,
            jnp.concatenate([partner_rows, portion], axis=axis_dim),
            jnp.concatenate([portion, partner_rows], axis=axis_dim),
        )
    return portion


def fetch_blocks(shard_rows, selector, geometry):
    device, group_bits, levels, block_rows = (geometry[0], geometry[1], geometry[2], geometry[3])
    own_panel = group_gather(shard_rows, 0, group_bits, device)
    selected = [pick_blocks(own_panel, lookup(selector, 0, device, geometry), block_rows)]
    for level_index in range(levels):
        bit_index = group_bits + level_index
        partner = device ^ 1 << bit_index
        wanted = pick_blocks(
            own_panel, lookup(selector, level_index + 1, partner, geometry), block_rows
        )
        selected.append(panel_trade(wanted, bit_index))
    return jnp.stack(selected)


def reduce_partials(contrib, selector, geometry):
    device, group_bits, levels, block_rows, panel_size = (
        geometry[0],
        geometry[1],
        geometry[2],
        geometry[3],
        geometry[7],
    )
    summed = place_blocks(contrib[0], lookup(selector, 0, device, geometry), block_rows, panel_size)
    for level_index in range(levels):
        bit_index = group_bits + level_index
        partner = device ^ 1 << bit_index
        arrived = partial_trade(contrib[level_index + 1], bit_index)
        summed = summed + place_blocks(
            arrived, lookup(selector, level_index + 1, partner, geometry), block_rows, panel_size
        )
    for bit_index in reversed(range(group_bits)):
        half_rows = summed.shape[0] // 2
        is_upper = device >> bit_index & 1 == 1
        kept_rows = jnp.where(is_upper, summed[half_rows:], summed[:half_rows])
        sent_rows = jnp.where(is_upper, summed[:half_rows], summed[half_rows:])
        summed = kept_rows + partial_trade(sent_rows, bit_index)
    return summed


def on_device(features, table_up, table_down, w_up, u_up, v_up, w_down, u_down, v_down, cotangent):
    device = lax.axis_index("tensor")
    slot_count, block_rows, hidden = w_up.shape
    levels = slot_count - 1
    group_bits = lax.axis_size("tensor").bit_length() - 1 - levels
    column_width = min(block_rows, hidden)
    block_count = hidden // column_width
    tokens_here = features.shape[1]
    panel_size = features.shape[0] * (1 << group_bits)
    geometry = (
        device,
        group_bits,
        levels,
        block_rows,
        hidden,
        column_width,
        block_count,
        panel_size,
    )
    up_blocks = w_up.reshape(slot_count, block_rows, block_count, column_width)
    down_blocks = w_down.reshape(slot_count, block_rows, block_count, column_width)
    a_up = lax.psum(jnp.dot(u_up.T, features, preferred_element_type=jnp.float32), "tensor")
    a_up_b = a_up.astype(jnp.bfloat16)
    picked_features = fetch_blocks(features, table_up, geometry)
    preact = jnp.einsum(
        "srbw,sbrt->bwt", up_blocks, picked_features, preferred_element_type=jnp.float32
    ).reshape(hidden, tokens_here)
    preact = preact + jnp.dot(v_up, a_up_b, preferred_element_type=jnp.float32)
    activation = gelu_value(preact).astype(jnp.bfloat16)
    a_down = lax.psum(jnp.dot(v_down.T, activation, preferred_element_type=jnp.float32), "tensor")
    a_down_b = a_down.astype(jnp.bfloat16)
    act_blocks = activation.reshape(block_count, column_width, tokens_here)
    partial_out = jnp.einsum(
        "srbw,bwt->sbrt", down_blocks, act_blocks, preferred_element_type=jnp.float32
    )
    output = (
        reduce_partials(partial_out, table_down, geometry)
        + jnp.dot(u_down, a_down_b, preferred_element_type=jnp.float32)
    ).astype(jnp.bfloat16)
    b_down = lax.psum(jnp.dot(u_down.T, cotangent, preferred_element_type=jnp.float32), "tensor")
    b_down_b = b_down.astype(jnp.bfloat16)
    picked_cotangent = fetch_blocks(cotangent, table_down, geometry)
    grad_act = jnp.einsum(
        "srbw,sbrt->bwt", down_blocks, picked_cotangent, preferred_element_type=jnp.float32
    ).reshape(hidden, tokens_here)
    grad_act = grad_act + jnp.dot(v_down, b_down_b, preferred_element_type=jnp.float32)
    grad_pre = (grad_act * gelu_slope(preact)).astype(jnp.bfloat16)
    grad_w_down = jnp.einsum(
        "sbrt,bwt->srbw", picked_cotangent, act_blocks, preferred_element_type=jnp.float32
    ).reshape(slot_count, block_rows, hidden)
    grad_u_down = jnp.dot(cotangent, a_down_b.T, preferred_element_type=jnp.float32)
    grad_v_down = jnp.dot(activation, b_down_b.T, preferred_element_type=jnp.float32)
    grad_w_down, grad_u_down, grad_v_down = (
        lax.psum_scatter(grad_w_down, "dp", scatter_dimension=1, tiled=True),
        lax.psum_scatter(grad_u_down, "dp", scatter_dimension=1, tiled=True),
        lax.psum_scatter(grad_v_down, "dp", scatter_dimension=1, tiled=True),
    )
    b_up = lax.psum(jnp.dot(v_up.T, grad_pre, preferred_element_type=jnp.float32), "tensor")
    b_up_b = b_up.astype(jnp.bfloat16)
    pre_blocks = grad_pre.reshape(block_count, column_width, tokens_here)
    partial_back = jnp.einsum(
        "srbw,bwt->sbrt", up_blocks, pre_blocks, preferred_element_type=jnp.float32
    )
    grad_features = (
        reduce_partials(partial_back, table_up, geometry)
        + jnp.dot(u_up, b_up_b, preferred_element_type=jnp.float32)
    ).astype(jnp.bfloat16)
    grad_w_up = jnp.einsum(
        "sbrt,bwt->srbw", picked_features, pre_blocks, preferred_element_type=jnp.float32
    ).reshape(slot_count, block_rows, hidden)
    grad_u_up = jnp.dot(features, b_up_b.T, preferred_element_type=jnp.float32)
    grad_v_up = jnp.dot(grad_pre, a_up_b.T, preferred_element_type=jnp.float32)
    grad_w_up, grad_u_up, grad_v_up = (
        lax.psum_scatter(grad_w_up, "dp", scatter_dimension=1, tiled=True),
        lax.psum_scatter(grad_u_up, "dp", scatter_dimension=1, tiled=True),
        lax.psum_scatter(grad_v_up, "dp", scatter_dimension=1, tiled=True),
    )
    return (
        output,
        grad_features,
        grad_w_up,
        grad_w_down,
        grad_u_up,
        grad_v_up,
        grad_u_down,
        grad_v_down,
    )


F32, BF16 = jnp.float32, jnp.bfloat16
VMEM_BYTES = 56 * 2**20


def nn(a, b):
    return lax.dot_general(a, b, (((1,), (0,)), ((), ())), preferred_element_type=F32)


def nt(a, b):
    return lax.dot_general(a, b, (((1,), (1,)), ((), ())), preferred_element_type=F32)


def tn(a, b):
    return lax.dot_general(a, b, (((0,), (0,)), ((), ())), preferred_element_type=F32)


def flip(me, offset):
    peer = me
    for k in range(offset.bit_length()):
        if offset >> k & 1:
            peer = peer + (1 << k) * (1 - 2 * ((me // (1 << k)) % 2))
    return peer


def remote(src, dst, send_sem, recv_sem, device_id):
    copy = pltpu.make_async_remote_copy(
        src_ref=src,
        dst_ref=dst,
        send_sem=send_sem,
        recv_sem=recv_sem,
        device_id=device_id,
        device_id_type=pl.DeviceIdType.MESH,
    )
    copy.start()
    return copy


def meet(n, me, half):
    barrier = pltpu.get_barrier_semaphore()
    for offset in range(1, n):
        pl.semaphore_signal(
            barrier,
            inc=1,
            device_id={"tensor": flip(me, offset)},
            device_id_type=pl.DeviceIdType.MESH,
        )
    count = n - 1
    if half is not None:
        pl.semaphore_signal(
            barrier, inc=1, device_id={"dp": 1 - half}, device_id_type=pl.DeviceIdType.MESH
        )
        count += 1
    pl.semaphore_wait(barrier, count)


def scatter_sums(n, me, part, slots, send, recv):
    rows = part.shape[1] // n
    copies = []
    for offset in range(1, n):
        peer = flip(me, offset)
        at = pl.ds(pl.multiple_of(peer * rows, rows), rows)
        copies.append(
            remote(
                part.at[:, at, :],
                slots.at[offset],
                send.at[0, offset],
                recv.at[0, offset],
                {"tensor": peer},
            )
        )
    return copies


def gather_sums(n, me, part, slots, total, send, recv, copies):
    rows = part.shape[1] // n
    mine = pl.ds(pl.multiple_of(me * rows, rows), rows)
    for copy in copies:
        copy.wait()
    summed = part[:, mine, :]
    for offset in range(1, n):
        summed = summed + slots[offset]
    total[:, mine, :] = summed.astype(BF16)
    return [
        remote(
            total.at[:, mine, :],
            total.at[:, mine, :],
            send.at[1, offset],
            recv.at[1, offset],
            {"tensor": flip(me, offset)},
        )
        for offset in range(1, n)
    ]


def fetch_kernel(
    n, levels, x_ref, c_ref, uu_ref, ud_ref, xg, cg, low, part, slots, send, recv, psend, precv
):
    me = lax.axis_index("tensor")
    meet(n, me, None)
    part[0] = tn(x_ref[...], uu_ref[...])
    part[1] = tn(c_ref[...], ud_ref[...])
    sums = scatter_sums(n, me, part, slots, send, recv)
    panels = []
    for level in reversed(range(levels)):
        for kind, (src, dst) in enumerate(((x_ref, xg), (c_ref, cg))):
            panels.append(
                remote(
                    src,
                    dst.at[level + 1],
                    psend.at[kind, level],
                    precv.at[kind, level],
                    {"tensor": flip(me, 1 << level)},
                )
            )
    xg[0] = x_ref[...]
    cg[0] = c_ref[...]
    rows = gather_sums(n, me, part, slots, low, send, recv, sums)
    for copy in panels + rows:
        copy.wait()


def fetch(n, levels, features, cotangent, u_up, u_down):
    dim, tokens = features.shape
    rank = u_up.shape[1]
    vmem = pl.BlockSpec(memory_space=pltpu.VMEM)
    return pl.pallas_call(
        functools.partial(fetch_kernel, n, levels),
        out_shape=(
            jax.ShapeDtypeStruct((levels + 1, dim, tokens), BF16),
            jax.ShapeDtypeStruct((levels + 1, dim, tokens), BF16),
            jax.ShapeDtypeStruct((2, tokens, rank), BF16),
        ),
        in_specs=[vmem] * 4,
        out_specs=(vmem,) * 3,
        scratch_shapes=[
            pltpu.VMEM((2, tokens, rank), F32),
            pltpu.VMEM((n, 2, tokens // n, rank), F32),
            pltpu.SemaphoreType.DMA((2, n)),
            pltpu.SemaphoreType.DMA((2, n)),
            pltpu.SemaphoreType.DMA((2, levels)),
            pltpu.SemaphoreType.DMA((2, levels)),
        ],
        compiler_params=pltpu.CompilerParams(
            collective_id=0, has_side_effects=True, vmem_limit_bytes=VMEM_BYTES
        ),
    )(features, cotangent, u_up, u_down)


def hidden_kernel(
    slot_count,
    block,
    steps,
    tables,
    xg,
    cg,
    low,
    wu,
    wd,
    vu,
    vd,
    act_out,
    pre_out,
    part,
    own,
    away,
    xt,
    ct,
    back,
):
    step = pl.program_id(0)
    per_panel = xg.shape[1] // block
    tokens = xg.shape[2]

    @pl.when(step == 0)
    def _():
        for slot in range(slot_count):
            for b in range(per_panel):
                rows = slice(b * block, (b + 1) * block)
                xt[slot, b] = xg[slot, rows, :].T
                ct[slot, b] = cg[slot, rows, :].T
        part[...] = jnp.zeros_like(part)
        back[...] = jnp.zeros_like(back)

    up = [tables[0, slot, step] for slot in range(slot_count)]
    down = [tables[1, slot, step] for slot in range(slot_count)]
    pre = nt(low[0], vu[...])
    grad = nt(low[1], vd[...])
    for slot in range(slot_count):
        pre = pre + nn(xt[slot, up[slot]], wu[slot])
        grad = grad + nn(ct[slot, down[slot]], wd[slot])
    cdf = 0.5 * (1.0 + lax.erf(pre * root_half))
    act = (pre * cdf).astype(BF16)
    grad_pre = (grad * (cdf + pre * jnp.exp(-0.5 * pre * pre) * inv_root_tau)).astype(BF16)
    act_out[...] = act
    pre_out[...] = grad_pre
    part[0] += nn(act, vd[...])
    part[1] += nn(grad_pre, vu[...])
    for slot in range(slot_count):
        back[slot, 0, down[slot]] += nt(wd[slot], act)
        back[slot, 1, up[slot]] += nt(wu[slot], grad_pre)

    @pl.when(step == steps - 1)
    def _():
        for kind in range(2):
            for b in range(per_panel):
                rows = slice(b * block, (b + 1) * block)
                own[kind, rows, :] = back[0, kind, b]
                for slot in range(1, slot_count):
                    away[slot - 1, kind, rows, :] = back[slot, kind, b].astype(BF16)


def hidden_pass(tables, xg, cg, low, w_up, w_down, v_up, v_down):
    slot_count, block, hidden = w_up.shape
    _, dim, tokens = xg.shape
    rank = v_up.shape[1]
    steps = hidden // block
    per_panel = dim // block
    whole = lambda *shape: pl.BlockSpec(shape, lambda c, *_: (0,) * len(shape))
    return pl.pallas_call(
        functools.partial(hidden_kernel, slot_count, block, steps),
        out_shape=(
            jax.ShapeDtypeStruct((tokens, hidden), BF16),
            jax.ShapeDtypeStruct((tokens, hidden), BF16),
            jax.ShapeDtypeStruct((2, tokens, rank), F32),
            jax.ShapeDtypeStruct((2, dim, tokens), F32),
            jax.ShapeDtypeStruct((slot_count - 1, 2, dim, tokens), BF16),
        ),
        grid_spec=pltpu.PrefetchScalarGridSpec(
            num_scalar_prefetch=1,
            grid=(steps,),
            in_specs=[
                whole(slot_count, dim, tokens),
                whole(slot_count, dim, tokens),
                whole(2, tokens, rank),
                pl.BlockSpec((slot_count, block, block), lambda c, *_: (0, 0, c)),
                pl.BlockSpec((slot_count, block, block), lambda c, *_: (0, 0, c)),
                pl.BlockSpec((block, rank), lambda c, *_: (c, 0)),
                pl.BlockSpec((block, rank), lambda c, *_: (c, 0)),
            ],
            out_specs=(
                pl.BlockSpec((tokens, block), lambda c, *_: (0, c)),
                pl.BlockSpec((tokens, block), lambda c, *_: (0, c)),
                whole(2, tokens, rank),
                whole(2, dim, tokens),
                whole(slot_count - 1, 2, dim, tokens),
            ),
            scratch_shapes=[
                pltpu.VMEM((slot_count, per_panel, tokens, block), BF16),
                pltpu.VMEM((slot_count, per_panel, tokens, block), BF16),
                pltpu.VMEM((slot_count, 2, per_panel, block, tokens), F32),
            ],
        ),
        compiler_params=pltpu.CompilerParams(vmem_limit_bytes=VMEM_BYTES),
    )(tables, xg, cg, low, w_up, w_down, v_up, v_down)


def return_kernel(
    n,
    levels,
    block,
    away,
    part_ref,
    act,
    pre,
    xg,
    cg,
    low_first,
    home,
    low,
    act_p,
    pre_p,
    x_p,
    c_p,
    xown_p,
    cown_p,
    lowf_p,
    low_p,
    slots,
    send,
    recv,
    psend,
    precv,
    dsend,
    drecv,
):
    me = lax.axis_index("tensor")
    half = lax.axis_index("dp")
    twin = {"dp": 1 - half}
    meet(n, me, half)
    sums = scatter_sums(n, me, part_ref, slots, send, recv)
    panels = []
    for level in reversed(range(levels)):
        panels.append(
            remote(
                away.at[level],
                home.at[level],
                psend.at[level],
                precv.at[level],
                {"tensor": flip(me, 1 << level)},
            )
        )
    rows = block // 2
    twins = []
    pairs = [(act, act_p), (pre, pre_p), (low_first, lowf_p), (xg.at[0], xown_p), (cg.at[0], cown_p)]
    for b in range(xg.shape[1] // block):
        at = pl.ds(pl.multiple_of(b * block + (1 - half) * rows, rows), rows)
        pairs.append((xg.at[:, at, :], x_p.at[:, b]))
        pairs.append((cg.at[:, at, :], c_p.at[:, b]))
    for k, (src, dst) in enumerate(pairs):
        twins.append(remote(src, dst, dsend.at[k], drecv.at[k], twin))
    gathered = gather_sums(n, me, part_ref, slots, low, send, recv, sums)
    for copy in gathered:
        copy.wait()
    last = len(pairs)
    twins.append(remote(low, low_p, dsend.at[last], drecv.at[last], twin))
    for copy in panels + twins:
        copy.wait()


def send_back(n, levels, block, away, part, act, pre, xg, cg, low_first):
    _, dim, tokens = xg.shape
    rank = part.shape[2]
    per_panel = dim // block
    vmem = pl.BlockSpec(memory_space=pltpu.VMEM)
    shape = lambda *s: jax.ShapeDtypeStruct(s, BF16)
    copies = 6 + 2 * per_panel
    return pl.pallas_call(
        functools.partial(return_kernel, n, levels, block),
        out_shape=(
            shape(*away.shape),
            shape(2, tokens, rank),
            shape(*act.shape),
            shape(*pre.shape),
            shape(levels + 1, per_panel, block // 2, tokens),
            shape(levels + 1, per_panel, block // 2, tokens),
            shape(dim, tokens),
            shape(dim, tokens),
            shape(2, tokens, rank),
            shape(2, tokens, rank),
        ),
        in_specs=[vmem] * 7,
        out_specs=(vmem,) * 10,
        scratch_shapes=[
            pltpu.VMEM((n, 2, tokens // n, rank), F32),
            pltpu.SemaphoreType.DMA((2, n)),
            pltpu.SemaphoreType.DMA((2, n)),
            pltpu.SemaphoreType.DMA((levels,)),
            pltpu.SemaphoreType.DMA((levels,)),
            pltpu.SemaphoreType.DMA((copies,)),
            pltpu.SemaphoreType.DMA((copies,)),
        ],
        compiler_params=pltpu.CompilerParams(
            collective_id=1, has_side_effects=True, vmem_limit_bytes=VMEM_BYTES
        ),
    )(away, part, act, pre, xg, cg, low_first)


def final_kernel(
    slot_count,
    block,
    tables,
    xg,
    cg,
    x_p,
    c_p,
    xown_p,
    cown_p,
    lowf,
    low,
    lowf_p,
    low_p,
    own,
    home,
    uu,
    ud,
    act,
    pre,
    act_p,
    pre_p,
    out,
    gfeat,
    gwu,
    gwd,
    guu,
    gvu,
    gud,
    gvd,
):
    step = pl.program_id(0)
    half = tables[2, 0, 0]
    rows = block // 2
    width = lowf.shape[2] // 2
    cols = pl.ds(pl.multiple_of(half * width, width), width)
    for slot in range(slot_count):
        for table, mine, twin, hid, hid_p, grad in (
            (0, xg, x_p, pre, pre_p, gwu),
            (1, cg, c_p, act, act_p, gwd),
        ):
            b = tables[table, slot, step]
            at = pl.ds(pl.multiple_of(b * block + half * rows, rows), rows)
            grad[slot] = nn(mine[slot, at, :], hid[...]) + nn(twin[slot, b], hid_p[...])
    gvu[...] = tn(pre[...], lowf[0, :, cols]) + tn(pre_p[...], lowf_p[0, :, cols])
    gvd[...] = tn(act[...], lowf[1, :, cols]) + tn(act_p[...], lowf_p[1, :, cols])

    @pl.when(step == 0)
    def _():
        for kind, u, result in ((0, ud, out), (1, uu, gfeat)):
            total = own[kind] + nt(u[...], low[kind])
            for level in range(slot_count - 1):
                total = total + home[level, kind].astype(F32)
            result[...] = total.astype(BF16)
        guu[...] = nn(xg[0], low[1, :, cols]) + nn(xown_p[...], low_p[1, :, cols])
        gud[...] = nn(cg[0], low[0, :, cols]) + nn(cown_p[...], low_p[0, :, cols])


def finish(tables, xg, cg, x_p, c_p, xown_p, cown_p, lowf, low, lowf_p, low_p, own, home, u_up, u_down,
           act, pre, act_p, pre_p, block):
    slot_count, dim, tokens = xg.shape
    hidden = act.shape[1]
    rank = lowf.shape[2]
    full = lambda a: pl.BlockSpec(a.shape, lambda c, *_: (0,) * a.ndim)
    hid = pl.BlockSpec((tokens, block), lambda c, *_: (0, c))
    gw = pl.BlockSpec((slot_count, block // 2, block), lambda c, *_: (0, 0, c))
    gv = pl.BlockSpec((block, rank // 2), lambda c, *_: (c, 0))
    once = lambda *shape: pl.BlockSpec(shape, lambda c, *_: (0,) * len(shape))
    fixed = (xg, cg, x_p, c_p, xown_p, cown_p, lowf, low, lowf_p, low_p, own, home, u_up, u_down)
    return pl.pallas_call(
        functools.partial(final_kernel, slot_count, block),
        out_shape=(
            jax.ShapeDtypeStruct((dim, tokens), BF16),
            jax.ShapeDtypeStruct((dim, tokens), BF16),
            jax.ShapeDtypeStruct((slot_count, block // 2, hidden), F32),
            jax.ShapeDtypeStruct((slot_count, block // 2, hidden), F32),
            jax.ShapeDtypeStruct((dim, rank // 2), F32),
            jax.ShapeDtypeStruct((hidden, rank // 2), F32),
            jax.ShapeDtypeStruct((dim, rank // 2), F32),
            jax.ShapeDtypeStruct((hidden, rank // 2), F32),
        ),
        grid_spec=pltpu.PrefetchScalarGridSpec(
            num_scalar_prefetch=1,
            grid=(hidden // block,),
            in_specs=[full(a) for a in fixed] + [hid] * 4,
            out_specs=(
                once(dim, tokens),
                once(dim, tokens),
                gw,
                gw,
                once(dim, rank // 2),
                gv,
                once(dim, rank // 2),
                gv,
            ),
        ),
        compiler_params=pltpu.CompilerParams(vmem_limit_bytes=VMEM_BYTES),
    )(tables, *fixed, act, pre, act_p, pre_p)


def one_panel_each(
    features, table_up, table_down, w_up, u_up, v_up, w_down, u_down, v_down, cotangent
):
    slot_count, block, hidden = w_up.shape
    levels = slot_count - 1
    n = lax.axis_size("tensor")
    me = lax.axis_index("tensor")
    count = hidden // block
    tables = lax.dynamic_slice_in_dim(jnp.stack([table_up, table_down]), me * count, count, 2)
    half = jnp.full((1,) + tables.shape[1:], lax.axis_index("dp"), jnp.int32)
    tables = jnp.concatenate([tables, half])
    xg, cg, lowf = fetch(n, levels, features, cotangent, u_up, u_down)
    act, pre, part, own, away = hidden_pass(tables, xg, cg, lowf, w_up, w_down, v_up, v_down)
    home, low, act_p, pre_p, x_p, c_p, xown_p, cown_p, lowf_p, low_p = send_back(
        n, levels, block, away, part, act, pre, xg, cg, lowf
    )
    return finish(tables, xg, cg, x_p, c_p, xown_p, cown_p, lowf, low, lowf_p, low_p, own, home,
                  u_up, u_down, act, pre, act_p, pre_p, block)


def solve(*args):
    slot_count = args[3].shape[0]
    fits = (
        lax.axis_size("tensor") == 1 << slot_count - 1
        and lax.axis_size("dp") == 2
        and args[3].shape[2] % args[3].shape[1] == 0
    )
    return one_panel_each(*args) if fits else on_device(*args)


def solution(mesh):
    return jax.shard_map(
        solve,
        mesh=mesh,
        in_specs=(
            P("tensor", ("groups", "dp")),
            P(),
            P(),
            P(None, None, "tensor"),
            P("tensor", None),
            P("tensor", None),
            P(None, None, "tensor"),
            P("tensor", None),
            P("tensor", None),
            P("tensor", ("groups", "dp")),
        ),
        out_specs=(
            P("tensor", ("groups", "dp")),
            P("tensor", ("groups", "dp")),
            P("groups", "dp", "tensor"),
            P("groups", "dp", "tensor"),
            P(("groups", "tensor"), "dp"),
            P(("groups", "tensor"), "dp"),
            P(("groups", "tensor"), "dp"),
            P(("groups", "tensor"), "dp"),
        ),
        check_vma=False,
    )
```

```python
import functools
import math

import jax
import jax.numpy as jnp
from jax import lax
from jax.experimental import pallas as pl
from jax.experimental.pallas import tpu as pltpu
from jax.sharding import PartitionSpec as P

root_half = 1.0 / math.sqrt(2.0)
inv_root_tau = 1.0 / math.sqrt(2.0 * math.pi)


def from_partner(array, axis, distance):
    return lax.ppermute(array, axis, [(i, i ^ 1 << distance) for i in range(lax.axis_size(axis))])


def gelu_value(values):
    return 0.5 * values * (1.0 + lax.erf(values * root_half))


def gelu_slope(values):
    return (
        0.5 * (1.0 + lax.erf(values * root_half))
        + values * jnp.exp(-0.5 * values * values) * inv_root_tau
    )


def panel_trade(values, bit_index):
    return from_partner(values, "tensor", bit_index)


def partial_trade(values, bit_index):
    return from_partner(values, "tensor", bit_index)


def block_ids(device, geometry):
    block_rows, hidden, column_width, block_count = (
        geometry[3],
        geometry[4],
        geometry[5],
        geometry[6],
    )
    starts = device * hidden + jnp.arange(block_count, dtype=jnp.int32) * column_width
    return starts // block_rows


def lookup(selector, slot_index, device, geometry):
    return jnp.take(selector[slot_index], block_ids(device, geometry), axis=0)


def pick_blocks(panel_rows, chosen, block_rows):
    stacked = panel_rows.reshape(panel_rows.shape[0] // block_rows, block_rows, panel_rows.shape[1])
    return jnp.take(stacked, chosen, axis=0)


def place_blocks(portion, chosen, block_rows, panel_size):
    per_panel = panel_size // block_rows
    onehot = (chosen[:, None] == jnp.arange(per_panel, dtype=jnp.int32)[None, :]).astype(
        jnp.float32
    )
    placed = jnp.einsum("bn,brt->nrt", onehot, portion, precision=lax.Precision.HIGHEST)
    return placed.reshape(panel_size, portion.shape[2])


def group_gather(portion, axis_dim, group_bits, device):
    for bit_index in range(group_bits):
        partner_rows = panel_trade(portion, bit_index)
        is_upper = device >> bit_index & 1 == 1
        portion = jnp.where(
            is_upper,
            jnp.concatenate([partner_rows, portion], axis=axis_dim),
            jnp.concatenate([portion, partner_rows], axis=axis_dim),
        )
    return portion


def fetch_blocks(shard_rows, selector, geometry):
    device, group_bits, levels, block_rows = (geometry[0], geometry[1], geometry[2], geometry[3])
    own_panel = group_gather(shard_rows, 0, group_bits, device)
    selected = [pick_blocks(own_panel, lookup(selector, 0, device, geometry), block_rows)]
    for level_index in range(levels):
        bit_index = group_bits + level_index
        partner = device ^ 1 << bit_index
        wanted = pick_blocks(
            own_panel, lookup(selector, level_index + 1, partner, geometry), block_rows
        )
        selected.append(panel_trade(wanted, bit_index))
    return jnp.stack(selected)


def reduce_partials(contrib, selector, geometry):
    device, group_bits, levels, block_rows, panel_size = (
        geometry[0],
        geometry[1],
        geometry[2],
        geometry[3],
        geometry[7],
    )
    summed = place_blocks(contrib[0], lookup(selector, 0, device, geometry), block_rows, panel_size)
    for level_index in range(levels):
        bit_index = group_bits + level_index
        partner = device ^ 1 << bit_index
        arrived = partial_trade(contrib[level_index + 1], bit_index)
        summed = summed + place_blocks(
            arrived, lookup(selector, level_index + 1, partner, geometry), block_rows, panel_size
        )
    for bit_index in reversed(range(group_bits)):
        half_rows = summed.shape[0] // 2
        is_upper = device >> bit_index & 1 == 1
        kept_rows = jnp.where(is_upper, summed[half_rows:], summed[:half_rows])
        sent_rows = jnp.where(is_upper, summed[:half_rows], summed[half_rows:])
        summed = kept_rows + partial_trade(sent_rows, bit_index)
    return summed


def on_device(features, table_up, table_down, w_up, u_up, v_up, w_down, u_down, v_down, cotangent):
    device = lax.axis_index("tensor")
    slot_count, block_rows, hidden = w_up.shape
    levels = slot_count - 1
    group_bits = lax.axis_size("tensor").bit_length() - 1 - levels
    column_width = min(block_rows, hidden)
    block_count = hidden // column_width
    tokens_here = features.shape[1]
    panel_size = features.shape[0] * (1 << group_bits)
    geometry = (
        device,
        group_bits,
        levels,
        block_rows,
        hidden,
        column_width,
        block_count,
        panel_size,
    )
    up_blocks = w_up.reshape(slot_count, block_rows, block_count, column_width)
    down_blocks = w_down.reshape(slot_count, block_rows, block_count, column_width)
    a_up = lax.psum(jnp.dot(u_up.T, features, preferred_element_type=jnp.float32), "tensor")
    a_up_b = a_up.astype(jnp.bfloat16)
    picked_features = fetch_blocks(features, table_up, geometry)
    preact = jnp.einsum(
        "srbw,sbrt->bwt", up_blocks, picked_features, preferred_element_type=jnp.float32
    ).reshape(hidden, tokens_here)
    preact = preact + jnp.dot(v_up, a_up_b, preferred_element_type=jnp.float32)
    activation = gelu_value(preact).astype(jnp.bfloat16)
    a_down = lax.psum(jnp.dot(v_down.T, activation, preferred_element_type=jnp.float32), "tensor")
    a_down_b = a_down.astype(jnp.bfloat16)
    act_blocks = activation.reshape(block_count, column_width, tokens_here)
    partial_out = jnp.einsum(
        "srbw,bwt->sbrt", down_blocks, act_blocks, preferred_element_type=jnp.float32
    )
    output = (
        reduce_partials(partial_out, table_down, geometry)
        + jnp.dot(u_down, a_down_b, preferred_element_type=jnp.float32)
    ).astype(jnp.bfloat16)
    b_down = lax.psum(jnp.dot(u_down.T, cotangent, preferred_element_type=jnp.float32), "tensor")
    b_down_b = b_down.astype(jnp.bfloat16)
    picked_cotangent = fetch_blocks(cotangent, table_down, geometry)
    grad_act = jnp.einsum(
        "srbw,sbrt->bwt", down_blocks, picked_cotangent, preferred_element_type=jnp.float32
    ).reshape(hidden, tokens_here)
    grad_act = grad_act + jnp.dot(v_down, b_down_b, preferred_element_type=jnp.float32)
    grad_pre = (grad_act * gelu_slope(preact)).astype(jnp.bfloat16)
    grad_w_down = jnp.einsum(
        "sbrt,bwt->srbw", picked_cotangent, act_blocks, preferred_element_type=jnp.float32
    ).reshape(slot_count, block_rows, hidden)
    grad_u_down = jnp.dot(cotangent, a_down_b.T, preferred_element_type=jnp.float32)
    grad_v_down = jnp.dot(activation, b_down_b.T, preferred_element_type=jnp.float32)
    grad_w_down, grad_u_down, grad_v_down = (
        lax.psum_scatter(grad_w_down, "dp", scatter_dimension=1, tiled=True),
        lax.psum_scatter(grad_u_down, "dp", scatter_dimension=1, tiled=True),
        lax.psum_scatter(grad_v_down, "dp", scatter_dimension=1, tiled=True),
    )
    b_up = lax.psum(jnp.dot(v_up.T, grad_pre, preferred_element_type=jnp.float32), "tensor")
    b_up_b = b_up.astype(jnp.bfloat16)
    pre_blocks = grad_pre.reshape(block_count, column_width, tokens_here)
    partial_back = jnp.einsum(
        "srbw,bwt->sbrt", up_blocks, pre_blocks, preferred_element_type=jnp.float32
    )
    grad_features = (
        reduce_partials(partial_back, table_up, geometry)
        + jnp.dot(u_up, b_up_b, preferred_element_type=jnp.float32)
    ).astype(jnp.bfloat16)
    grad_w_up = jnp.einsum(
        "sbrt,bwt->srbw", picked_features, pre_blocks, preferred_element_type=jnp.float32
    ).reshape(slot_count, block_rows, hidden)
    grad_u_up = jnp.dot(features, b_up_b.T, preferred_element_type=jnp.float32)
    grad_v_up = jnp.dot(grad_pre, a_up_b.T, preferred_element_type=jnp.float32)
    grad_w_up, grad_u_up, grad_v_up = (
        lax.psum_scatter(grad_w_up, "dp", scatter_dimension=1, tiled=True),
        lax.psum_scatter(grad_u_up, "dp", scatter_dimension=1, tiled=True),
        lax.psum_scatter(grad_v_up, "dp", scatter_dimension=1, tiled=True),
    )
    return (
        output,
        grad_features,
        grad_w_up,
        grad_w_down,
        grad_u_up,
        grad_v_up,
        grad_u_down,
        grad_v_down,
    )


F32, BF16 = jnp.float32, jnp.bfloat16
VMEM_BYTES = 56 * 2**20


def nn(a, b):
    return lax.dot_general(a, b, (((1,), (0,)), ((), ())), preferred_element_type=F32)


def nt(a, b):
    return lax.dot_general(a, b, (((1,), (1,)), ((), ())), preferred_element_type=F32)


def tn(a, b):
    return lax.dot_general(a, b, (((0,), (0,)), ((), ())), preferred_element_type=F32)


def flip(me, offset):
    peer = me
    for k in range(offset.bit_length()):
        if offset >> k & 1:
            peer = peer + (1 << k) * (1 - 2 * ((me // (1 << k)) % 2))
    return peer


def remote(src, dst, send_sem, recv_sem, device_id):
    copy = pltpu.make_async_remote_copy(
        src_ref=src,
        dst_ref=dst,
        send_sem=send_sem,
        recv_sem=recv_sem,
        device_id=device_id,
        device_id_type=pl.DeviceIdType.MESH,
    )
    copy.start()
    return copy


def meet(n, me, half):
    barrier = pltpu.get_barrier_semaphore()
    for offset in range(1, n):
        pl.semaphore_signal(
            barrier,
            inc=1,
            device_id={"tensor": flip(me, offset)},
            device_id_type=pl.DeviceIdType.MESH,
        )
    count = n - 1
    if half is not None:
        pl.semaphore_signal(
            barrier, inc=1, device_id={"dp": 1 - half}, device_id_type=pl.DeviceIdType.MESH
        )
        count += 1
    pl.semaphore_wait(barrier, count)


def scatter_sums(n, me, part, rounded, slots, send, recv):
    group = n // 2
    rows = part.shape[1] // group
    rounded[...] = part[...].astype(BF16)
    copies = []
    for offset in range(1, group):
        peer = flip(me, offset)
        at = pl.ds(pl.multiple_of(peer % group * rows, rows), rows)
        copies.append(
            remote(
                rounded.at[:, at, :],
                slots.at[offset],
                send.at[0, offset],
                recv.at[0, offset],
                {"tensor": peer},
            )
        )
    return copies


def cross_sums(n, me, part, slots, pair, send, recv, copies):
    group = n // 2
    rows = part.shape[1] // group
    mine = pl.ds(pl.multiple_of(me % group * rows, rows), rows)
    for copy in copies:
        copy.wait()
    summed = part[:, mine, :]
    for offset in range(1, group):
        summed = summed + slots[offset].astype(F32)
    pair[0] = summed.astype(BF16)
    return remote(
        pair.at[0], pair.at[1], send.at[0, 0], recv.at[0, 0], {"tensor": flip(me, group)}
    )


def gather_sums(n, me, pair, total, send, recv, copy):
    group = n // 2
    rows = pair.shape[2]
    mine = pl.ds(pl.multiple_of(me % group * rows, rows), rows)
    copy.wait()
    total[:, mine, :] = (pair[0].astype(F32) + pair[1].astype(F32)).astype(BF16)
    return [
        remote(
            total.at[:, mine, :],
            total.at[:, mine, :],
            send.at[1, offset],
            recv.at[1, offset],
            {"tensor": flip(me, offset)},
        )
        for offset in range(1, group)
    ]


def sum_scratch(n, tokens, rank):
    group = n // 2
    return [
        pltpu.VMEM((2, tokens, rank), BF16),
        pltpu.VMEM((group, 2, tokens // group, rank), BF16),
        pltpu.VMEM((2, 2, tokens // group, rank), BF16),
        pltpu.SemaphoreType.DMA((2, group)),
        pltpu.SemaphoreType.DMA((2, group)),
    ]


def fetch_kernel(
    n, levels, x_ref, c_ref, uu_ref, ud_ref, xg, cg, low, part, rounded, slots, pair, send, recv, psend, precv
):
    me = lax.axis_index("tensor")
    meet(n, me, None)
    part[0] = tn(x_ref[...], uu_ref[...])
    part[1] = tn(c_ref[...], ud_ref[...])
    sums = scatter_sums(n, me, part, rounded, slots, send, recv)
    panels = []
    for level in reversed(range(levels)):
        for kind, (src, dst) in enumerate(((x_ref, xg), (c_ref, cg))):
            panels.append(
                remote(
                    src,
                    dst.at[level + 1],
                    psend.at[kind, level],
                    precv.at[kind, level],
                    {"tensor": flip(me, 1 << level)},
                )
            )
    xg[0] = x_ref[...]
    cg[0] = c_ref[...]
    crossing = cross_sums(n, me, part, slots, pair, send, recv, sums)
    rows = gather_sums(n, me, pair, low, send, recv, crossing)
    for copy in panels + rows:
        copy.wait()


def fetch(n, levels, features, cotangent, u_up, u_down):
    dim, tokens = features.shape
    rank = u_up.shape[1]
    vmem = pl.BlockSpec(memory_space=pltpu.VMEM)
    return pl.pallas_call(
        functools.partial(fetch_kernel, n, levels),
        out_shape=(
            jax.ShapeDtypeStruct((levels + 1, dim, tokens), BF16),
            jax.ShapeDtypeStruct((levels + 1, dim, tokens), BF16),
            jax.ShapeDtypeStruct((2, tokens, rank), BF16),
        ),
        in_specs=[vmem] * 4,
        out_specs=(vmem,) * 3,
        scratch_shapes=[
            pltpu.VMEM((2, tokens, rank), F32),
            *sum_scratch(n, tokens, rank),
            pltpu.SemaphoreType.DMA((2, levels)),
            pltpu.SemaphoreType.DMA((2, levels)),
        ],
        compiler_params=pltpu.CompilerParams(
            collective_id=0, has_side_effects=True, vmem_limit_bytes=VMEM_BYTES
        ),
    )(features, cotangent, u_up, u_down)


def hidden_kernel(
    slot_count,
    block,
    steps,
    tables,
    xg,
    cg,
    low,
    wu,
    wd,
    vu,
    vd,
    act_out,
    pre_out,
    part,
    own,
    away,
    xt,
    ct,
    back,
):
    step = pl.program_id(0)
    per_panel = xg.shape[1] // block
    tokens = xg.shape[2]

    @pl.when(step == 0)
    def _():
        for slot in range(slot_count):
            for b in range(per_panel):
                rows = slice(b * block, (b + 1) * block)
                xt[slot, b] = xg[slot, rows, :].T
                ct[slot, b] = cg[slot, rows, :].T
        part[...] = jnp.zeros_like(part)
        back[...] = jnp.zeros_like(back)

    up = [tables[0, slot, step] for slot in range(slot_count)]
    down = [tables[1, slot, step] for slot in range(slot_count)]
    pre = nt(low[0], vu[...])
    grad = nt(low[1], vd[...])
    for slot in range(slot_count):
        pre = pre + nn(xt[slot, up[slot]], wu[slot])
        grad = grad + nn(ct[slot, down[slot]], wd[slot])
    cdf = 0.5 * (1.0 + lax.erf(pre * root_half))
    act = (pre * cdf).astype(BF16)
    grad_pre = (grad * (cdf + pre * jnp.exp(-0.5 * pre * pre) * inv_root_tau)).astype(BF16)
    act_out[...] = act
    pre_out[...] = grad_pre
    part[0] += nn(act, vd[...])
    part[1] += nn(grad_pre, vu[...])
    for slot in range(slot_count):
        back[slot, 0, down[slot]] += nt(wd[slot], act)
        back[slot, 1, up[slot]] += nt(wu[slot], grad_pre)

    @pl.when(step == steps - 1)
    def _():
        for kind in range(2):
            for b in range(per_panel):
                rows = slice(b * block, (b + 1) * block)
                own[kind, rows, :] = back[0, kind, b]
                for slot in range(1, slot_count):
                    away[slot - 1, kind, rows, :] = back[slot, kind, b].astype(BF16)


def hidden_pass(tables, xg, cg, low, w_up, w_down, v_up, v_down):
    slot_count, block, hidden = w_up.shape
    _, dim, tokens = xg.shape
    rank = v_up.shape[1]
    steps = hidden // block
    per_panel = dim // block
    whole = lambda *shape: pl.BlockSpec(shape, lambda c, *_: (0,) * len(shape))
    return pl.pallas_call(
        functools.partial(hidden_kernel, slot_count, block, steps),
        out_shape=(
            jax.ShapeDtypeStruct((tokens, hidden), BF16),
            jax.ShapeDtypeStruct((tokens, hidden), BF16),
            jax.ShapeDtypeStruct((2, tokens, rank), F32),
            jax.ShapeDtypeStruct((2, dim, tokens), F32),
            jax.ShapeDtypeStruct((slot_count - 1, 2, dim, tokens), BF16),
        ),
        grid_spec=pltpu.PrefetchScalarGridSpec(
            num_scalar_prefetch=1,
            grid=(steps,),
            in_specs=[
                whole(slot_count, dim, tokens),
                whole(slot_count, dim, tokens),
                whole(2, tokens, rank),
                pl.BlockSpec((slot_count, block, block), lambda c, *_: (0, 0, c)),
                pl.BlockSpec((slot_count, block, block), lambda c, *_: (0, 0, c)),
                pl.BlockSpec((block, rank), lambda c, *_: (c, 0)),
                pl.BlockSpec((block, rank), lambda c, *_: (c, 0)),
            ],
            out_specs=(
                pl.BlockSpec((tokens, block), lambda c, *_: (0, c)),
                pl.BlockSpec((tokens, block), lambda c, *_: (0, c)),
                whole(2, tokens, rank),
                whole(2, dim, tokens),
                whole(slot_count - 1, 2, dim, tokens),
            ),
            scratch_shapes=[
                pltpu.VMEM((slot_count, per_panel, tokens, block), BF16),
                pltpu.VMEM((slot_count, per_panel, tokens, block), BF16),
                pltpu.VMEM((slot_count, 2, per_panel, block, tokens), F32),
            ],
        ),
        compiler_params=pltpu.CompilerParams(vmem_limit_bytes=VMEM_BYTES),
    )(tables, xg, cg, low, w_up, w_down, v_up, v_down)


def return_kernel(
    n,
    levels,
    block,
    away,
    part_ref,
    act,
    pre,
    xg,
    cg,
    low_first,
    home,
    low,
    act_p,
    pre_p,
    x_p,
    c_p,
    xown_p,
    cown_p,
    lowf_p,
    low_p,
    rounded,
    slots,
    pair,
    send,
    recv,
    psend,
    precv,
    dsend,
    drecv,
):
    me = lax.axis_index("tensor")
    half = lax.axis_index("dp")
    twin = {"dp": 1 - half}
    meet(n, me, half)
    sums = scatter_sums(n, me, part_ref, rounded, slots, send, recv)
    panels = []
    for level in reversed(range(levels)):
        panels.append(
            remote(
                away.at[level],
                home.at[level],
                psend.at[level],
                precv.at[level],
                {"tensor": flip(me, 1 << level)},
            )
        )
    rows = block // 2
    twins = []
    pairs = [(act, act_p), (pre, pre_p), (low_first, lowf_p), (xg.at[0], xown_p), (cg.at[0], cown_p)]
    for b in range(xg.shape[1] // block):
        at = pl.ds(pl.multiple_of(b * block + (1 - half) * rows, rows), rows)
        pairs.append((xg.at[:, at, :], x_p.at[:, b]))
        pairs.append((cg.at[:, at, :], c_p.at[:, b]))
    for k, (src, dst) in enumerate(pairs):
        twins.append(remote(src, dst, dsend.at[k], drecv.at[k], twin))
    crossing = cross_sums(n, me, part_ref, slots, pair, send, recv, sums)
    gathered = gather_sums(n, me, pair, low, send, recv, crossing)
    for copy in gathered:
        copy.wait()
    last = len(pairs)
    twins.append(remote(low, low_p, dsend.at[last], drecv.at[last], twin))
    for copy in panels + twins:
        copy.wait()


def send_back(n, levels, block, away, part, act, pre, xg, cg, low_first):
    _, dim, tokens = xg.shape
    rank = part.shape[2]
    per_panel = dim // block
    vmem = pl.BlockSpec(memory_space=pltpu.VMEM)
    shape = lambda *s: jax.ShapeDtypeStruct(s, BF16)
    copies = 6 + 2 * per_panel
    return pl.pallas_call(
        functools.partial(return_kernel, n, levels, block),
        out_shape=(
            shape(*away.shape),
            shape(2, tokens, rank),
            shape(*act.shape),
            shape(*pre.shape),
            shape(levels + 1, per_panel, block // 2, tokens),
            shape(levels + 1, per_panel, block // 2, tokens),
            shape(dim, tokens),
            shape(dim, tokens),
            shape(2, tokens, rank),
            shape(2, tokens, rank),
        ),
        in_specs=[vmem] * 7,
        out_specs=(vmem,) * 10,
        scratch_shapes=[
            *sum_scratch(n, tokens, rank),
            pltpu.SemaphoreType.DMA((levels,)),
            pltpu.SemaphoreType.DMA((levels,)),
            pltpu.SemaphoreType.DMA((copies,)),
            pltpu.SemaphoreType.DMA((copies,)),
        ],
        compiler_params=pltpu.CompilerParams(
            collective_id=1, has_side_effects=True, vmem_limit_bytes=VMEM_BYTES
        ),
    )(away, part, act, pre, xg, cg, low_first)


def final_kernel(
    slot_count,
    block,
    tables,
    xg,
    cg,
    x_p,
    c_p,
    xown_p,
    cown_p,
    lowf,
    low,
    lowf_p,
    low_p,
    own,
    home,
    uu,
    ud,
    act,
    pre,
    act_p,
    pre_p,
    out,
    gfeat,
    gwu,
    gwd,
    guu,
    gvu,
    gud,
    gvd,
):
    step = pl.program_id(0)
    half = tables[2, 0, 0]
    rows = block // 2
    width = lowf.shape[2] // 2
    cols = pl.ds(pl.multiple_of(half * width, width), width)
    for slot in range(slot_count):
        for table, mine, twin, hid, hid_p, grad in (
            (0, xg, x_p, pre, pre_p, gwu),
            (1, cg, c_p, act, act_p, gwd),
        ):
            b = tables[table, slot, step]
            at = pl.ds(pl.multiple_of(b * block + half * rows, rows), rows)
            grad[slot] = nn(mine[slot, at, :], hid[...]) + nn(twin[slot, b], hid_p[...])
    gvu[...] = tn(pre[...], lowf[0, :, cols]) + tn(pre_p[...], lowf_p[0, :, cols])
    gvd[...] = tn(act[...], lowf[1, :, cols]) + tn(act_p[...], lowf_p[1, :, cols])

    @pl.when(step == 0)
    def _():
        for kind, u, result in ((0, ud, out), (1, uu, gfeat)):
            total = own[kind] + nt(u[...], low[kind])
            for level in range(slot_count - 1):
                total = total + home[level, kind].astype(F32)
            result[...] = total.astype(BF16)
        guu[...] = nn(xg[0], low[1, :, cols]) + nn(xown_p[...], low_p[1, :, cols])
        gud[...] = nn(cg[0], low[0, :, cols]) + nn(cown_p[...], low_p[0, :, cols])


def finish(tables, xg, cg, x_p, c_p, xown_p, cown_p, lowf, low, lowf_p, low_p, own, home, u_up, u_down,
           act, pre, act_p, pre_p, block):
    slot_count, dim, tokens = xg.shape
    hidden = act.shape[1]
    rank = lowf.shape[2]
    full = lambda a: pl.BlockSpec(a.shape, lambda c, *_: (0,) * a.ndim)
    hid = pl.BlockSpec((tokens, block), lambda c, *_: (0, c))
    gw = pl.BlockSpec((slot_count, block // 2, block), lambda c, *_: (0, 0, c))
    gv = pl.BlockSpec((block, rank // 2), lambda c, *_: (c, 0))
    once = lambda *shape: pl.BlockSpec(shape, lambda c, *_: (0,) * len(shape))
    fixed = (xg, cg, x_p, c_p, xown_p, cown_p, lowf, low, lowf_p, low_p, own, home, u_up, u_down)
    return pl.pallas_call(
        functools.partial(final_kernel, slot_count, block),
        out_shape=(
            jax.ShapeDtypeStruct((dim, tokens), BF16),
            jax.ShapeDtypeStruct((dim, tokens), BF16),
            jax.ShapeDtypeStruct((slot_count, block // 2, hidden), F32),
            jax.ShapeDtypeStruct((slot_count, block // 2, hidden), F32),
            jax.ShapeDtypeStruct((dim, rank // 2), F32),
            jax.ShapeDtypeStruct((hidden, rank // 2), F32),
            jax.ShapeDtypeStruct((dim, rank // 2), F32),
            jax.ShapeDtypeStruct((hidden, rank // 2), F32),
        ),
        grid_spec=pltpu.PrefetchScalarGridSpec(
            num_scalar_prefetch=1,
            grid=(hidden // block,),
            in_specs=[full(a) for a in fixed] + [hid] * 4,
            out_specs=(
                once(dim, tokens),
                once(dim, tokens),
                gw,
                gw,
                once(dim, rank // 2),
                gv,
                once(dim, rank // 2),
                gv,
            ),
        ),
        compiler_params=pltpu.CompilerParams(vmem_limit_bytes=VMEM_BYTES),
    )(tables, *fixed, act, pre, act_p, pre_p)


def one_panel_each(
    features, table_up, table_down, w_up, u_up, v_up, w_down, u_down, v_down, cotangent
):
    slot_count, block, hidden = w_up.shape
    levels = slot_count - 1
    n = lax.axis_size("tensor")
    me = lax.axis_index("tensor")
    count = hidden // block
    tables = lax.dynamic_slice_in_dim(jnp.stack([table_up, table_down]), me * count, count, 2)
    half = jnp.full((1,) + tables.shape[1:], lax.axis_index("dp"), jnp.int32)
    tables = jnp.concatenate([tables, half])
    xg, cg, lowf = fetch(n, levels, features, cotangent, u_up, u_down)
    act, pre, part, own, away = hidden_pass(tables, xg, cg, lowf, w_up, w_down, v_up, v_down)
    home, low, act_p, pre_p, x_p, c_p, xown_p, cown_p, lowf_p, low_p = send_back(
        n, levels, block, away, part, act, pre, xg, cg, lowf
    )
    return finish(tables, xg, cg, x_p, c_p, xown_p, cown_p, lowf, low, lowf_p, low_p, own, home,
                  u_up, u_down, act, pre, act_p, pre_p, block)


def solve(*args):
    slot_count = args[3].shape[0]
    fits = (
        slot_count > 1
        and lax.axis_size("tensor") == 1 << slot_count - 1
        and lax.axis_size("dp") == 2
        and args[3].shape[2] % args[3].shape[1] == 0
    )
    return one_panel_each(*args) if fits else on_device(*args)


def solution(mesh):
    return jax.shard_map(
        solve,
        mesh=mesh,
        in_specs=(
            P("tensor", ("groups", "dp")),
            P(),
            P(),
            P(None, None, "tensor"),
            P("tensor", None),
            P("tensor", None),
            P(None, None, "tensor"),
            P("tensor", None),
            P("tensor", None),
            P("tensor", ("groups", "dp")),
        ),
        out_specs=(
            P("tensor", ("groups", "dp")),
            P("tensor", ("groups", "dp")),
            P("groups", "dp", "tensor"),
            P("groups", "dp", "tensor"),
            P(("groups", "tensor"), "dp"),
            P(("groups", "tensor"), "dp"),
            P(("groups", "tensor"), "dp"),
            P(("groups", "tensor"), "dp"),
        ),
        check_vma=False,
    )
```

```python
import functools
import math

import jax
import jax.numpy as jnp
from jax import lax
from jax.experimental import pallas as pl
from jax.experimental.pallas import tpu as pltpu
from jax.sharding import PartitionSpec as P

root_half = 1.0 / math.sqrt(2.0)
inv_root_tau = 1.0 / math.sqrt(2.0 * math.pi)


def from_partner(array, axis, distance):
    return lax.ppermute(array, axis, [(i, i ^ 1 << distance) for i in range(lax.axis_size(axis))])


def gelu_value(values):
    return 0.5 * values * (1.0 + lax.erf(values * root_half))


def gelu_slope(values):
    return (
        0.5 * (1.0 + lax.erf(values * root_half))
        + values * jnp.exp(-0.5 * values * values) * inv_root_tau
    )


def panel_trade(values, bit_index):
    return from_partner(values, "tensor", bit_index)


def partial_trade(values, bit_index):
    return from_partner(values, "tensor", bit_index)


def block_ids(device, geometry):
    block_rows, hidden, column_width, block_count = (
        geometry[3],
        geometry[4],
        geometry[5],
        geometry[6],
    )
    starts = device * hidden + jnp.arange(block_count, dtype=jnp.int32) * column_width
    return starts // block_rows


def lookup(selector, slot_index, device, geometry):
    return jnp.take(selector[slot_index], block_ids(device, geometry), axis=0)


def pick_blocks(panel_rows, chosen, block_rows):
    stacked = panel_rows.reshape(panel_rows.shape[0] // block_rows, block_rows, panel_rows.shape[1])
    return jnp.take(stacked, chosen, axis=0)


def place_blocks(portion, chosen, block_rows, panel_size):
    per_panel = panel_size // block_rows
    onehot = (chosen[:, None] == jnp.arange(per_panel, dtype=jnp.int32)[None, :]).astype(
        jnp.float32
    )
    placed = jnp.einsum("bn,brt->nrt", onehot, portion, precision=lax.Precision.HIGHEST)
    return placed.reshape(panel_size, portion.shape[2])


def group_gather(portion, axis_dim, group_bits, device):
    for bit_index in range(group_bits):
        partner_rows = panel_trade(portion, bit_index)
        is_upper = device >> bit_index & 1 == 1
        portion = jnp.where(
            is_upper,
            jnp.concatenate([partner_rows, portion], axis=axis_dim),
            jnp.concatenate([portion, partner_rows], axis=axis_dim),
        )
    return portion


def fetch_blocks(shard_rows, selector, geometry):
    device, group_bits, levels, block_rows = (geometry[0], geometry[1], geometry[2], geometry[3])
    own_panel = group_gather(shard_rows, 0, group_bits, device)
    selected = [pick_blocks(own_panel, lookup(selector, 0, device, geometry), block_rows)]
    for level_index in range(levels):
        bit_index = group_bits + level_index
        partner = device ^ 1 << bit_index
        wanted = pick_blocks(
            own_panel, lookup(selector, level_index + 1, partner, geometry), block_rows
        )
        selected.append(panel_trade(wanted, bit_index))
    return jnp.stack(selected)


def reduce_partials(contrib, selector, geometry):
    device, group_bits, levels, block_rows, panel_size = (
        geometry[0],
        geometry[1],
        geometry[2],
        geometry[3],
        geometry[7],
    )
    summed = place_blocks(contrib[0], lookup(selector, 0, device, geometry), block_rows, panel_size)
    for level_index in range(levels):
        bit_index = group_bits + level_index
        partner = device ^ 1 << bit_index
        arrived = partial_trade(contrib[level_index + 1], bit_index)
        summed = summed + place_blocks(
            arrived, lookup(selector, level_index + 1, partner, geometry), block_rows, panel_size
        )
    for bit_index in reversed(range(group_bits)):
        half_rows = summed.shape[0] // 2
        is_upper = device >> bit_index & 1 == 1
        kept_rows = jnp.where(is_upper, summed[half_rows:], summed[:half_rows])
        sent_rows = jnp.where(is_upper, summed[:half_rows], summed[half_rows:])
        summed = kept_rows + partial_trade(sent_rows, bit_index)
    return summed


def on_device(features, table_up, table_down, w_up, u_up, v_up, w_down, u_down, v_down, cotangent):
    device = lax.axis_index("tensor")
    slot_count, block_rows, hidden = w_up.shape
    levels = slot_count - 1
    group_bits = lax.axis_size("tensor").bit_length() - 1 - levels
    column_width = min(block_rows, hidden)
    block_count = hidden // column_width
    tokens_here = features.shape[1]
    panel_size = features.shape[0] * (1 << group_bits)
    geometry = (
        device,
        group_bits,
        levels,
        block_rows,
        hidden,
        column_width,
        block_count,
        panel_size,
    )
    up_blocks = w_up.reshape(slot_count, block_rows, block_count, column_width)
    down_blocks = w_down.reshape(slot_count, block_rows, block_count, column_width)
    a_up = lax.psum(jnp.dot(u_up.T, features, preferred_element_type=jnp.float32), "tensor")
    a_up_b = a_up.astype(jnp.bfloat16)
    picked_features = fetch_blocks(features, table_up, geometry)
    preact = jnp.einsum(
        "srbw,sbrt->bwt", up_blocks, picked_features, preferred_element_type=jnp.float32
    ).reshape(hidden, tokens_here)
    preact = preact + jnp.dot(v_up, a_up_b, preferred_element_type=jnp.float32)
    activation = gelu_value(preact).astype(jnp.bfloat16)
    a_down = lax.psum(jnp.dot(v_down.T, activation, preferred_element_type=jnp.float32), "tensor")
    a_down_b = a_down.astype(jnp.bfloat16)
    act_blocks = activation.reshape(block_count, column_width, tokens_here)
    partial_out = jnp.einsum(
        "srbw,bwt->sbrt", down_blocks, act_blocks, preferred_element_type=jnp.float32
    )
    output = (
        reduce_partials(partial_out, table_down, geometry)
        + jnp.dot(u_down, a_down_b, preferred_element_type=jnp.float32)
    ).astype(jnp.bfloat16)
    b_down = lax.psum(jnp.dot(u_down.T, cotangent, preferred_element_type=jnp.float32), "tensor")
    b_down_b = b_down.astype(jnp.bfloat16)
    picked_cotangent = fetch_blocks(cotangent, table_down, geometry)
    grad_act = jnp.einsum(
        "srbw,sbrt->bwt", down_blocks, picked_cotangent, preferred_element_type=jnp.float32
    ).reshape(hidden, tokens_here)
    grad_act = grad_act + jnp.dot(v_down, b_down_b, preferred_element_type=jnp.float32)
    grad_pre = (grad_act * gelu_slope(preact)).astype(jnp.bfloat16)
    grad_w_down = jnp.einsum(
        "sbrt,bwt->srbw", picked_cotangent, act_blocks, preferred_element_type=jnp.float32
    ).reshape(slot_count, block_rows, hidden)
    grad_u_down = jnp.dot(cotangent, a_down_b.T, preferred_element_type=jnp.float32)
    grad_v_down = jnp.dot(activation, b_down_b.T, preferred_element_type=jnp.float32)
    grad_w_down, grad_u_down, grad_v_down = (
        lax.psum_scatter(grad_w_down, "dp", scatter_dimension=1, tiled=True),
        lax.psum_scatter(grad_u_down, "dp", scatter_dimension=1, tiled=True),
        lax.psum_scatter(grad_v_down, "dp", scatter_dimension=1, tiled=True),
    )
    b_up = lax.psum(jnp.dot(v_up.T, grad_pre, preferred_element_type=jnp.float32), "tensor")
    b_up_b = b_up.astype(jnp.bfloat16)
    pre_blocks = grad_pre.reshape(block_count, column_width, tokens_here)
    partial_back = jnp.einsum(
        "srbw,bwt->sbrt", up_blocks, pre_blocks, preferred_element_type=jnp.float32
    )
    grad_features = (
        reduce_partials(partial_back, table_up, geometry)
        + jnp.dot(u_up, b_up_b, preferred_element_type=jnp.float32)
    ).astype(jnp.bfloat16)
    grad_w_up = jnp.einsum(
        "sbrt,bwt->srbw", picked_features, pre_blocks, preferred_element_type=jnp.float32
    ).reshape(slot_count, block_rows, hidden)
    grad_u_up = jnp.dot(features, b_up_b.T, preferred_element_type=jnp.float32)
    grad_v_up = jnp.dot(grad_pre, a_up_b.T, preferred_element_type=jnp.float32)
    grad_w_up, grad_u_up, grad_v_up = (
        lax.psum_scatter(grad_w_up, "dp", scatter_dimension=1, tiled=True),
        lax.psum_scatter(grad_u_up, "dp", scatter_dimension=1, tiled=True),
        lax.psum_scatter(grad_v_up, "dp", scatter_dimension=1, tiled=True),
    )
    return (
        output,
        grad_features,
        grad_w_up,
        grad_w_down,
        grad_u_up,
        grad_v_up,
        grad_u_down,
        grad_v_down,
    )


F32, BF16 = jnp.float32, jnp.bfloat16
VMEM_BYTES = 56 * 2**20


def nn(a, b):
    return lax.dot_general(a, b, (((1,), (0,)), ((), ())), preferred_element_type=F32)


def nt(a, b):
    return lax.dot_general(a, b, (((1,), (1,)), ((), ())), preferred_element_type=F32)


def tn(a, b):
    return lax.dot_general(a, b, (((0,), (0,)), ((), ())), preferred_element_type=F32)


def flip(me, offset):
    peer = me
    for k in range(offset.bit_length()):
        if offset >> k & 1:
            peer = peer + (1 << k) * (1 - 2 * ((me // (1 << k)) % 2))
    return peer


def remote(src, dst, send_sem, recv_sem, device_id):
    copy = pltpu.make_async_remote_copy(
        src_ref=src,
        dst_ref=dst,
        send_sem=send_sem,
        recv_sem=recv_sem,
        device_id=device_id,
        device_id_type=pl.DeviceIdType.MESH,
    )
    copy.start()
    return copy


def meet(n, me, half):
    barrier = pltpu.get_barrier_semaphore()
    for offset in range(1, n):
        pl.semaphore_signal(
            barrier,
            inc=1,
            device_id={"tensor": flip(me, offset)},
            device_id_type=pl.DeviceIdType.MESH,
        )
    count = n - 1
    if half is not None:
        pl.semaphore_signal(
            barrier, inc=1, device_id={"dp": 1 - half}, device_id_type=pl.DeviceIdType.MESH
        )
        count += 1
    pl.semaphore_wait(barrier, count)


def scatter_sums(n, me, part, slots, send, recv):
    group = n // 2
    rows = part.shape[1] // group
    copies = []
    for offset in range(1, group):
        peer = flip(me, offset)
        at = pl.ds(pl.multiple_of(peer % group * rows, rows), rows)
        copies.append(
            remote(
                part.at[:, at, :],
                slots.at[offset],
                send.at[0, offset],
                recv.at[0, offset],
                {"tensor": peer},
            )
        )
    return copies


def cross_sums(n, me, part, slots, pair, send, recv, copies):
    group = n // 2
    rows = part.shape[1] // group
    mine = pl.ds(pl.multiple_of(me % group * rows, rows), rows)
    for copy in copies:
        copy.wait()
    summed = part[:, mine, :]
    for offset in range(1, group):
        summed = summed + slots[offset]
    pair[0] = summed
    return remote(
        pair.at[0], pair.at[1], send.at[0, 0], recv.at[0, 0], {"tensor": flip(me, group)}
    )


def gather_sums(n, me, pair, total, send, recv, copy):
    group = n // 2
    rows = pair.shape[2]
    mine = pl.ds(pl.multiple_of(me % group * rows, rows), rows)
    copy.wait()
    total[:, mine, :] = (pair[0] + pair[1]).astype(BF16)
    return [
        remote(
            total.at[:, mine, :],
            total.at[:, mine, :],
            send.at[1, offset],
            recv.at[1, offset],
            {"tensor": flip(me, offset)},
        )
        for offset in range(1, group)
    ]


def sum_scratch(n, lead, tokens, rank):
    group = n // 2
    return [
        pltpu.VMEM((lead, tokens, rank), F32),
        pltpu.VMEM((group, lead, tokens // group, rank), F32),
        pltpu.VMEM((2, lead, tokens // group, rank), F32),
        pltpu.SemaphoreType.DMA((2, group)),
        pltpu.SemaphoreType.DMA((2, group)),
    ]


def layer_kernel(n, levels, block, tables, x_ref, c_ref, uu, ud, wu_any, wd_any, vu_any, vd_any, *refs):
    (xg, cg, lowf, act, pre, own, home, low_a, low_b, act_p, pre_p, x_p, c_p) = refs[:13]
    (xown_p, cown_p, lowf_p, lowa_p, lowb_p) = refs[13:18]
    first, second, third = refs[18:23], refs[23:28], refs[28:33]
    (wu, wd, vu, vd, xt, ct, slope, acc, away, lsem, psend, precv, dsend, drecv) = refs[33:]
    me = lax.axis_index("tensor")
    half = lax.axis_index("dp")
    twin = {"dp": 1 - half}
    slot_count = levels + 1
    per_panel = x_ref.shape[0] // block
    steps = act.shape[1] // block
    loads = []
    for k, (src, dst) in enumerate(((wu_any, wu), (vu_any, vu), (wd_any, wd), (vd_any, vd))):
        loads.append(pltpu.make_async_copy(src, dst, lsem.at[k]))
        loads[-1].start()
    meet(n, me, half)

    def to_partner(src, dst, kind, level):
        return remote(
            src,
            dst,
            psend.at[kind, level],
            precv.at[kind, level],
            {"tensor": flip(me, 1 << level)},
        )

    twins = []

    def to_twin(src, dst):
        k = len(twins)
        twins.append(remote(src, dst, dsend.at[k], drecv.at[k], twin))

    def halves_to_twin(rows_ref, dst):
        rows = block // 2
        for b in range(per_panel):
            at = pl.ds(pl.multiple_of(b * block + (1 - half) * rows, rows), rows)
            to_twin(rows_ref.at[:, at, :], dst.at[:, b])

    def turn(panels, turned, slot):
        for b in range(per_panel):
            turned[slot, b] = panels[slot, b * block : (b + 1) * block, :].T

    order = tuple(reversed(range(levels)))
    xs = {level: to_partner(x_ref, xg.at[level + 1], 0, level) for level in order}
    to_twin(x_ref, xown_p)
    to_twin(c_ref, cown_p)
    part, slots, pair, send, recv = first
    part[0] = tn(x_ref[...], uu[...])
    part[1] = tn(c_ref[...], ud[...])
    sums = scatter_sums(n, me, part, slots, send, recv)
    xg[0] = x_ref[...]
    cg[0] = c_ref[...]
    turn(xg, xt, 0)
    turn(cg, ct, 0)
    acc[...] = jnp.zeros_like(acc)
    second[0][...] = jnp.zeros_like(second[0])
    third[0][...] = jnp.zeros_like(third[0])
    crossing = cross_sums(n, me, part, slots, pair, send, recv, sums)
    rows = gather_sums(n, me, pair, lowf, send, recv, crossing)
    cs = {}
    for level in range(levels):
        xs[level].wait()
        cs[level] = to_partner(c_ref, cg.at[level + 1], 1, level)
        turn(xg, xt, level + 1)
    halves_to_twin(xg, x_p)
    for copy in rows:
        copy.wait()
    to_twin(lowf, lowf_p)
    for load in loads:
        load.wait()

    def add_blocks(kind, table, step, weights, hidden):
        cols = pl.ds(pl.multiple_of(step * block, block), block)
        for slot in range(slot_count):
            term = nt(weights[slot, :, cols], hidden)
            for b in range(per_panel):
                here = (tables[table, slot, step] == b).astype(F32)
                acc[slot, kind, b] += term * here

    def forward(step, carry):
        cols = pl.ds(pl.multiple_of(step * block, block), block)
        values = nt(lowf[0], vu[cols, :])
        for slot in range(slot_count):
            values = values + nn(xt[slot, tables[0, slot, step]], wu[slot, :, cols])
        cdf = 0.5 * (1.0 + lax.erf(values * root_half))
        slope[:, cols] = cdf + values * jnp.exp(-0.5 * values * values) * inv_root_tau
        hidden = (values * cdf).astype(BF16)
        act[:, cols] = hidden
        second[0][0] += nn(hidden, vd[cols, :])
        add_blocks(0, 1, step, wd, hidden)
        return carry

    def backward(step, carry):
        cols = pl.ds(pl.multiple_of(step * block, block), block)
        values = nt(lowf[1], vd[cols, :])
        for slot in range(slot_count):
            values = values + nn(ct[slot, tables[1, slot, step]], wd[slot, :, cols])
        hidden = (values * slope[:, cols]).astype(BF16)
        pre[:, cols] = hidden
        third[0][0] += nn(hidden, vu[cols, :])
        add_blocks(1, 0, step, wu, hidden)
        return carry

    def hand_on(kind):
        copies = []
        for level in order:
            for b in range(per_panel):
                at = slice(b * block, (b + 1) * block)
                away[level, kind, at, :] = acc[level + 1, kind, b].astype(BF16)
            copies.append(to_partner(away.at[level, kind], home.at[level, kind], 2 + kind, level))
        for b in range(per_panel):
            own[kind, b * block : (b + 1) * block, :] = acc[0, kind, b]
        return copies

    lax.fori_loop(0, steps, forward, 0)
    part_a, slots_a, pair_a, send_a, recv_a = second
    sums_a = scatter_sums(n, me, part_a, slots_a, send_a, recv_a)
    partials = hand_on(0)
    to_twin(act, act_p)
    for level in cs:
        cs[level].wait()
        turn(cg, ct, level + 1)
    halves_to_twin(cg, c_p)
    crossing_a = cross_sums(n, me, part_a, slots_a, pair_a, send_a, recv_a, sums_a)
    lax.fori_loop(0, steps, backward, 0)
    part_b, slots_b, pair_b, send_b, recv_b = third
    sums_b = scatter_sums(n, me, part_b, slots_b, send_b, recv_b)
    partials = partials + hand_on(1)
    to_twin(pre, pre_p)
    rows_a = gather_sums(n, me, pair_a, low_a, send_a, recv_a, crossing_a)
    crossing_b = cross_sums(n, me, part_b, slots_b, pair_b, send_b, recv_b, sums_b)
    rows_b = gather_sums(n, me, pair_b, low_b, send_b, recv_b, crossing_b)
    for copy in rows_a:
        copy.wait()
    to_twin(low_a, lowa_p)
    for copy in rows_b:
        copy.wait()
    to_twin(low_b, lowb_p)
    for copy in partials + twins:
        copy.wait()


def layer(tables, features, cotangent, u_up, u_down, w_up, w_down, v_up, v_down, n):
    slot_count, block, hidden = w_up.shape
    levels = slot_count - 1
    dim, tokens = features.shape
    rank = u_up.shape[1]
    per_panel = dim // block
    vmem = pl.BlockSpec(memory_space=pltpu.VMEM)
    far = pl.BlockSpec(memory_space=pl.ANY)
    b16 = lambda *s: jax.ShapeDtypeStruct(s, BF16)
    copies = 7 + 2 * per_panel
    return pl.pallas_call(
        functools.partial(layer_kernel, n, levels, block),
        out_shape=(
            b16(slot_count, dim, tokens),
            b16(slot_count, dim, tokens),
            b16(2, tokens, rank),
            b16(tokens, hidden),
            b16(tokens, hidden),
            jax.ShapeDtypeStruct((2, dim, tokens), F32),
            b16(levels, 2, dim, tokens),
            b16(1, tokens, rank),
            b16(1, tokens, rank),
            b16(tokens, hidden),
            b16(tokens, hidden),
            b16(slot_count, per_panel, block // 2, tokens),
            b16(slot_count, per_panel, block // 2, tokens),
            b16(dim, tokens),
            b16(dim, tokens),
            b16(2, tokens, rank),
            b16(1, tokens, rank),
            b16(1, tokens, rank),
        ),
        in_specs=[pl.BlockSpec(memory_space=pltpu.SMEM)] + [vmem] * 4 + [far] * 4,
        out_specs=(vmem,) * 18,
        scratch_shapes=[
            *sum_scratch(n, 2, tokens, rank),
            *sum_scratch(n, 1, tokens, rank),
            *sum_scratch(n, 1, tokens, rank),
            pltpu.VMEM(w_up.shape, BF16),
            pltpu.VMEM(w_down.shape, BF16),
            pltpu.VMEM(v_up.shape, BF16),
            pltpu.VMEM(v_down.shape, BF16),
            pltpu.VMEM((slot_count, per_panel, tokens, block), BF16),
            pltpu.VMEM((slot_count, per_panel, tokens, block), BF16),
            pltpu.VMEM((tokens, hidden), F32),
            pltpu.VMEM((slot_count, 2, per_panel, block, tokens), F32),
            pltpu.VMEM((levels, 2, dim, tokens), BF16),
            pltpu.SemaphoreType.DMA((4,)),
            pltpu.SemaphoreType.DMA((4, levels)),
            pltpu.SemaphoreType.DMA((4, levels)),
            pltpu.SemaphoreType.DMA((copies,)),
            pltpu.SemaphoreType.DMA((copies,)),
        ],
        compiler_params=pltpu.CompilerParams(
            collective_id=0, has_side_effects=True, vmem_limit_bytes=VMEM_BYTES
        ),
    )(tables, features, cotangent, u_up, u_down, w_up, w_down, v_up, v_down)


def final_kernel(
    slot_count,
    block,
    tables,
    xg,
    cg,
    x_p,
    c_p,
    xown_p,
    cown_p,
    lowf,
    low_a,
    low_b,
    lowf_p,
    lowa_p,
    lowb_p,
    own,
    home,
    uu,
    ud,
    act,
    pre,
    act_p,
    pre_p,
    out,
    gfeat,
    gwu,
    gwd,
    guu,
    gvu,
    gud,
    gvd,
):
    step = pl.program_id(0)
    half = tables[2, 0, 0]
    rows = block // 2
    width = lowf.shape[2] // 2
    cols = pl.ds(pl.multiple_of(half * width, width), width)
    for slot in range(slot_count):
        for table, mine, twin, hid, hid_p, grad in (
            (0, xg, x_p, pre, pre_p, gwu),
            (1, cg, c_p, act, act_p, gwd),
        ):
            b = tables[table, slot, step]
            at = pl.ds(pl.multiple_of(b * block + half * rows, rows), rows)
            grad[slot] = nn(mine[slot, at, :], hid[...]) + nn(twin[slot, b], hid_p[...])
    gvu[...] = tn(pre[...], lowf[0, :, cols]) + tn(pre_p[...], lowf_p[0, :, cols])
    gvd[...] = tn(act[...], lowf[1, :, cols]) + tn(act_p[...], lowf_p[1, :, cols])

    @pl.when(step == 0)
    def _():
        for kind, u, low, result in ((0, ud, low_a, out), (1, uu, low_b, gfeat)):
            total = own[kind] + nt(u[...], low[0])
            for level in range(slot_count - 1):
                total = total + home[level, kind].astype(F32)
            result[...] = total.astype(BF16)
        guu[...] = nn(xg[0], low_b[0, :, cols]) + nn(xown_p[...], lowb_p[0, :, cols])
        gud[...] = nn(cg[0], low_a[0, :, cols]) + nn(cown_p[...], lowa_p[0, :, cols])


def finish(tables, xg, cg, x_p, c_p, xown_p, cown_p, lowf, low_a, low_b, lowf_p, lowa_p, lowb_p, own, home, u_up, u_down,
           act, pre, act_p, pre_p, block):
    slot_count, dim, tokens = xg.shape
    hidden = act.shape[1]
    rank = lowf.shape[2]
    full = lambda a: pl.BlockSpec(a.shape, lambda c, *_: (0,) * a.ndim)
    hid = pl.BlockSpec((tokens, block), lambda c, *_: (0, c))
    gw = pl.BlockSpec((slot_count, block // 2, block), lambda c, *_: (0, 0, c))
    gv = pl.BlockSpec((block, rank // 2), lambda c, *_: (c, 0))
    once = lambda *shape: pl.BlockSpec(shape, lambda c, *_: (0,) * len(shape))
    fixed = (xg, cg, x_p, c_p, xown_p, cown_p, lowf, low_a, low_b, lowf_p, lowa_p, lowb_p, own, home, u_up, u_down)
    return pl.pallas_call(
        functools.partial(final_kernel, slot_count, block),
        out_shape=(
            jax.ShapeDtypeStruct((dim, tokens), BF16),
            jax.ShapeDtypeStruct((dim, tokens), BF16),
            jax.ShapeDtypeStruct((slot_count, block // 2, hidden), F32),
            jax.ShapeDtypeStruct((slot_count, block // 2, hidden), F32),
            jax.ShapeDtypeStruct((dim, rank // 2), F32),
            jax.ShapeDtypeStruct((hidden, rank // 2), F32),
            jax.ShapeDtypeStruct((dim, rank // 2), F32),
            jax.ShapeDtypeStruct((hidden, rank // 2), F32),
        ),
        grid_spec=pltpu.PrefetchScalarGridSpec(
            num_scalar_prefetch=1,
            grid=(hidden // block,),
            in_specs=[full(a) for a in fixed] + [hid] * 4,
            out_specs=(
                once(dim, tokens),
                once(dim, tokens),
                gw,
                gw,
                once(dim, rank // 2),
                gv,
                once(dim, rank // 2),
                gv,
            ),
        ),
        compiler_params=pltpu.CompilerParams(vmem_limit_bytes=VMEM_BYTES),
    )(tables, *fixed, act, pre, act_p, pre_p)


def one_panel_each(
    features, table_up, table_down, w_up, u_up, v_up, w_down, u_down, v_down, cotangent
):
    slot_count, block, hidden = w_up.shape
    levels = slot_count - 1
    n = lax.axis_size("tensor")
    me = lax.axis_index("tensor")
    count = hidden // block
    tables = lax.dynamic_slice_in_dim(jnp.stack([table_up, table_down]), me * count, count, 2)
    half = jnp.full((1,) + tables.shape[1:], lax.axis_index("dp"), jnp.int32)
    tables = jnp.concatenate([tables, half])
    (xg, cg, lowf, act, pre, own, home, low_a, low_b, act_p, pre_p, x_p, c_p, xown_p, cown_p, lowf_p,
     lowa_p, lowb_p) = layer(
        tables, features, cotangent, u_up, u_down, w_up, w_down, v_up, v_down, n
    )
    return finish(tables, xg, cg, x_p, c_p, xown_p, cown_p, lowf, low_a, low_b, lowf_p, lowa_p, lowb_p,
                  own, home, u_up, u_down, act, pre, act_p, pre_p, block)


def solve(*args):
    slot_count = args[3].shape[0]
    fits = (
        slot_count > 1
        and lax.axis_size("tensor") == 1 << slot_count - 1
        and lax.axis_size("dp") == 2
        and args[3].shape[2] % args[3].shape[1] == 0
    )
    return one_panel_each(*args) if fits else on_device(*args)


def solution(mesh):
    return jax.shard_map(
        solve,
        mesh=mesh,
        in_specs=(
            P("tensor", ("groups", "dp")),
            P(),
            P(),
            P(None, None, "tensor"),
            P("tensor", None),
            P("tensor", None),
            P(None, None, "tensor"),
            P("tensor", None),
            P("tensor", None),
            P("tensor", ("groups", "dp")),
        ),
        out_specs=(
            P("tensor", ("groups", "dp")),
            P("tensor", ("groups", "dp")),
            P("groups", "dp", "tensor"),
            P("groups", "dp", "tensor"),
            P(("groups", "tensor"), "dp"),
            P(("groups", "tensor"), "dp"),
            P(("groups", "tensor"), "dp"),
            P(("groups", "tensor"), "dp"),
        ),
        check_vma=False,
    )
```

```python
import functools
import math

import jax
import jax.numpy as jnp
from jax import lax
from jax.experimental import pallas as pl
from jax.experimental.pallas import tpu as pltpu
from jax.sharding import PartitionSpec as P

root_half = 1.0 / math.sqrt(2.0)
inv_root_tau = 1.0 / math.sqrt(2.0 * math.pi)


def from_partner(array, axis, distance):
    return lax.ppermute(array, axis, [(i, i ^ 1 << distance) for i in range(lax.axis_size(axis))])


def gelu_value(values):
    return 0.5 * values * (1.0 + lax.erf(values * root_half))


def gelu_slope(values):
    return (
        0.5 * (1.0 + lax.erf(values * root_half))
        + values * jnp.exp(-0.5 * values * values) * inv_root_tau
    )


def panel_trade(values, bit_index):
    return from_partner(values, "tensor", bit_index)


def partial_trade(values, bit_index):
    return from_partner(values, "tensor", bit_index)


def block_ids(device, geometry):
    block_rows, hidden, column_width, block_count = (
        geometry[3],
        geometry[4],
        geometry[5],
        geometry[6],
    )
    starts = device * hidden + jnp.arange(block_count, dtype=jnp.int32) * column_width
    return starts // block_rows


def lookup(selector, slot_index, device, geometry):
    return jnp.take(selector[slot_index], block_ids(device, geometry), axis=0)


def pick_blocks(panel_rows, chosen, block_rows):
    stacked = panel_rows.reshape(panel_rows.shape[0] // block_rows, block_rows, panel_rows.shape[1])
    return jnp.take(stacked, chosen, axis=0)


def place_blocks(portion, chosen, block_rows, panel_size):
    per_panel = panel_size // block_rows
    onehot = (chosen[:, None] == jnp.arange(per_panel, dtype=jnp.int32)[None, :]).astype(
        jnp.float32
    )
    placed = jnp.einsum("bn,brt->nrt", onehot, portion, precision=lax.Precision.HIGHEST)
    return placed.reshape(panel_size, portion.shape[2])


def group_gather(portion, axis_dim, group_bits, device):
    for bit_index in range(group_bits):
        partner_rows = panel_trade(portion, bit_index)
        is_upper = device >> bit_index & 1 == 1
        portion = jnp.where(
            is_upper,
            jnp.concatenate([partner_rows, portion], axis=axis_dim),
            jnp.concatenate([portion, partner_rows], axis=axis_dim),
        )
    return portion


def fetch_blocks(shard_rows, selector, geometry):
    device, group_bits, levels, block_rows = (geometry[0], geometry[1], geometry[2], geometry[3])
    own_panel = group_gather(shard_rows, 0, group_bits, device)
    selected = [pick_blocks(own_panel, lookup(selector, 0, device, geometry), block_rows)]
    for level_index in range(levels):
        bit_index = group_bits + level_index
        partner = device ^ 1 << bit_index
        wanted = pick_blocks(
            own_panel, lookup(selector, level_index + 1, partner, geometry), block_rows
        )
        selected.append(panel_trade(wanted, bit_index))
    return jnp.stack(selected)


def reduce_partials(contrib, selector, geometry):
    device, group_bits, levels, block_rows, panel_size = (
        geometry[0],
        geometry[1],
        geometry[2],
        geometry[3],
        geometry[7],
    )
    summed = place_blocks(contrib[0], lookup(selector, 0, device, geometry), block_rows, panel_size)
    for level_index in range(levels):
        bit_index = group_bits + level_index
        partner = device ^ 1 << bit_index
        arrived = partial_trade(contrib[level_index + 1], bit_index)
        summed = summed + place_blocks(
            arrived, lookup(selector, level_index + 1, partner, geometry), block_rows, panel_size
        )
    for bit_index in reversed(range(group_bits)):
        half_rows = summed.shape[0] // 2
        is_upper = device >> bit_index & 1 == 1
        kept_rows = jnp.where(is_upper, summed[half_rows:], summed[:half_rows])
        sent_rows = jnp.where(is_upper, summed[:half_rows], summed[half_rows:])
        summed = kept_rows + partial_trade(sent_rows, bit_index)
    return summed


def on_device(features, table_up, table_down, w_up, u_up, v_up, w_down, u_down, v_down, cotangent):
    device = lax.axis_index("tensor")
    slot_count, block_rows, hidden = w_up.shape
    levels = slot_count - 1
    group_bits = lax.axis_size("tensor").bit_length() - 1 - levels
    column_width = min(block_rows, hidden)
    block_count = hidden // column_width
    tokens_here = features.shape[1]
    panel_size = features.shape[0] * (1 << group_bits)
    geometry = (
        device,
        group_bits,
        levels,
        block_rows,
        hidden,
        column_width,
        block_count,
        panel_size,
    )
    up_blocks = w_up.reshape(slot_count, block_rows, block_count, column_width)
    down_blocks = w_down.reshape(slot_count, block_rows, block_count, column_width)
    a_up = lax.psum(jnp.dot(u_up.T, features, preferred_element_type=jnp.float32), "tensor")
    a_up_b = a_up.astype(jnp.bfloat16)
    picked_features = fetch_blocks(features, table_up, geometry)
    preact = jnp.einsum(
        "srbw,sbrt->bwt", up_blocks, picked_features, preferred_element_type=jnp.float32
    ).reshape(hidden, tokens_here)
    preact = preact + jnp.dot(v_up, a_up_b, preferred_element_type=jnp.float32)
    activation = gelu_value(preact).astype(jnp.bfloat16)
    a_down = lax.psum(jnp.dot(v_down.T, activation, preferred_element_type=jnp.float32), "tensor")
    a_down_b = a_down.astype(jnp.bfloat16)
    act_blocks = activation.reshape(block_count, column_width, tokens_here)
    partial_out = jnp.einsum(
        "srbw,bwt->sbrt", down_blocks, act_blocks, preferred_element_type=jnp.float32
    )
    output = (
        reduce_partials(partial_out, table_down, geometry)
        + jnp.dot(u_down, a_down_b, preferred_element_type=jnp.float32)
    ).astype(jnp.bfloat16)
    b_down = lax.psum(jnp.dot(u_down.T, cotangent, preferred_element_type=jnp.float32), "tensor")
    b_down_b = b_down.astype(jnp.bfloat16)
    picked_cotangent = fetch_blocks(cotangent, table_down, geometry)
    grad_act = jnp.einsum(
        "srbw,sbrt->bwt", down_blocks, picked_cotangent, preferred_element_type=jnp.float32
    ).reshape(hidden, tokens_here)
    grad_act = grad_act + jnp.dot(v_down, b_down_b, preferred_element_type=jnp.float32)
    grad_pre = (grad_act * gelu_slope(preact)).astype(jnp.bfloat16)
    grad_w_down = jnp.einsum(
        "sbrt,bwt->srbw", picked_cotangent, act_blocks, preferred_element_type=jnp.float32
    ).reshape(slot_count, block_rows, hidden)
    grad_u_down = jnp.dot(cotangent, a_down_b.T, preferred_element_type=jnp.float32)
    grad_v_down = jnp.dot(activation, b_down_b.T, preferred_element_type=jnp.float32)
    grad_w_down, grad_u_down, grad_v_down = (
        lax.psum_scatter(grad_w_down, "dp", scatter_dimension=1, tiled=True),
        lax.psum_scatter(grad_u_down, "dp", scatter_dimension=1, tiled=True),
        lax.psum_scatter(grad_v_down, "dp", scatter_dimension=1, tiled=True),
    )
    b_up = lax.psum(jnp.dot(v_up.T, grad_pre, preferred_element_type=jnp.float32), "tensor")
    b_up_b = b_up.astype(jnp.bfloat16)
    pre_blocks = grad_pre.reshape(block_count, column_width, tokens_here)
    partial_back = jnp.einsum(
        "srbw,bwt->sbrt", up_blocks, pre_blocks, preferred_element_type=jnp.float32
    )
    grad_features = (
        reduce_partials(partial_back, table_up, geometry)
        + jnp.dot(u_up, b_up_b, preferred_element_type=jnp.float32)
    ).astype(jnp.bfloat16)
    grad_w_up = jnp.einsum(
        "sbrt,bwt->srbw", picked_features, pre_blocks, preferred_element_type=jnp.float32
    ).reshape(slot_count, block_rows, hidden)
    grad_u_up = jnp.dot(features, b_up_b.T, preferred_element_type=jnp.float32)
    grad_v_up = jnp.dot(grad_pre, a_up_b.T, preferred_element_type=jnp.float32)
    grad_w_up, grad_u_up, grad_v_up = (
        lax.psum_scatter(grad_w_up, "dp", scatter_dimension=1, tiled=True),
        lax.psum_scatter(grad_u_up, "dp", scatter_dimension=1, tiled=True),
        lax.psum_scatter(grad_v_up, "dp", scatter_dimension=1, tiled=True),
    )
    return (
        output,
        grad_features,
        grad_w_up,
        grad_w_down,
        grad_u_up,
        grad_v_up,
        grad_u_down,
        grad_v_down,
    )


F32, BF16 = jnp.float32, jnp.bfloat16
VMEM_BYTES = 56 * 2**20


def nn(a, b):
    return lax.dot_general(a, b, (((1,), (0,)), ((), ())), preferred_element_type=F32)


def nt(a, b):
    return lax.dot_general(a, b, (((1,), (1,)), ((), ())), preferred_element_type=F32)


def tn(a, b):
    return lax.dot_general(a, b, (((0,), (0,)), ((), ())), preferred_element_type=F32)


def flip(me, offset):
    peer = me
    for k in range(offset.bit_length()):
        if offset >> k & 1:
            peer = peer + (1 << k) * (1 - 2 * ((me // (1 << k)) % 2))
    return peer


def remote(src, dst, send_sem, recv_sem, device_id):
    copy = pltpu.make_async_remote_copy(
        src_ref=src,
        dst_ref=dst,
        send_sem=send_sem,
        recv_sem=recv_sem,
        device_id=device_id,
        device_id_type=pl.DeviceIdType.MESH,
    )
    copy.start()
    return copy


def meet(n, me, half):
    barrier = pltpu.get_barrier_semaphore()
    for offset in range(1, n):
        pl.semaphore_signal(
            barrier,
            inc=1,
            device_id={"tensor": flip(me, offset)},
            device_id_type=pl.DeviceIdType.MESH,
        )
    count = n - 1
    if half is not None:
        pl.semaphore_signal(
            barrier, inc=1, device_id={"dp": 1 - half}, device_id_type=pl.DeviceIdType.MESH
        )
        count += 1
    pl.semaphore_wait(barrier, count)


def scatter_sums(n, me, part, slots, send, recv):
    group = n // 2
    rows = part.shape[1] // group
    copies = []
    for offset in range(1, group):
        peer = flip(me, offset)
        at = pl.ds(pl.multiple_of(peer % group * rows, rows), rows)
        copies.append(
            remote(
                part.at[:, at, :],
                slots.at[offset],
                send.at[0, offset],
                recv.at[0, offset],
                {"tensor": peer},
            )
        )
    return copies


def cross_sums(n, me, part, slots, pair, send, recv, copies):
    group = n // 2
    rows = part.shape[1] // group
    mine = pl.ds(pl.multiple_of(me % group * rows, rows), rows)
    for copy in copies:
        copy.wait()
    summed = part[:, mine, :]
    for offset in range(1, group):
        summed = summed + slots[offset]
    pair[0] = summed
    return remote(
        pair.at[0], pair.at[1], send.at[0, 0], recv.at[0, 0], {"tensor": flip(me, group)}
    )


def gather_sums(n, me, pair, total, send, recv, copy):
    group = n // 2
    rows = pair.shape[2]
    mine = pl.ds(pl.multiple_of(me % group * rows, rows), rows)
    copy.wait()
    total[:, mine, :] = (pair[0] + pair[1]).astype(BF16)
    return [
        remote(
            total.at[:, mine, :],
            total.at[:, mine, :],
            send.at[1, offset],
            recv.at[1, offset],
            {"tensor": flip(me, offset)},
        )
        for offset in range(1, group)
    ]


def sum_scratch(n, lead, tokens, rank):
    group = n // 2
    return [
        pltpu.VMEM((lead, tokens, rank), F32),
        pltpu.VMEM((group, lead, tokens // group, rank), F32),
        pltpu.VMEM((2, lead, tokens // group, rank), F32),
        pltpu.SemaphoreType.DMA((2, group)),
        pltpu.SemaphoreType.DMA((2, group)),
    ]


def layer_kernel(n, levels, block, table_up, table_down, x_ref, c_ref, uu, ud, wu_any, wd_any, vu_any, vd_any, *refs):
    (xg, cg, lowf, act, pre, own, home, low_a, low_b, act_p, pre_p, x_p, c_p) = refs[:13]
    (xown_p, cown_p, lowf_p, lowa_p, lowb_p) = refs[13:18]
    first, second, third = refs[18:23], refs[23:28], refs[28:33]
    (wu, wd, vu, vd, xt, ct, slope, acc, away, lsem, psend, precv, dsend, drecv) = refs[33:]
    me = lax.axis_index("tensor")
    half = lax.axis_index("dp")
    twin = {"dp": 1 - half}
    slot_count = levels + 1
    per_panel = x_ref.shape[0] // block
    steps = act.shape[1] // block
    tables = (table_up, table_down)
    base = me * steps
    loads = []
    for k, (src, dst) in enumerate(((wu_any, wu), (vu_any, vu), (wd_any, wd), (vd_any, vd))):
        loads.append(pltpu.make_async_copy(src, dst, lsem.at[k]))
        loads[-1].start()
    meet(n, me, half)

    def to_partner(src, dst, kind, level):
        return remote(
            src,
            dst,
            psend.at[kind, level],
            precv.at[kind, level],
            {"tensor": flip(me, 1 << level)},
        )

    twins = []

    def to_twin(src, dst):
        k = len(twins)
        twins.append(remote(src, dst, dsend.at[k], drecv.at[k], twin))

    def halves_to_twin(rows_ref, dst):
        rows = block // 2
        for b in range(per_panel):
            at = pl.ds(pl.multiple_of(b * block + (1 - half) * rows, rows), rows)
            to_twin(rows_ref.at[:, at, :], dst.at[:, b])

    def turn(panels, turned, slot):
        for b in range(per_panel):
            turned[slot, b] = panels[slot, b * block : (b + 1) * block, :].T

    order = tuple(reversed(range(levels)))
    xs = {level: to_partner(x_ref, xg.at[level + 1], 0, level) for level in order}
    to_twin(x_ref, xown_p)
    to_twin(c_ref, cown_p)
    part, slots, pair, send, recv = first
    part[0] = tn(x_ref[...], uu[...])
    part[1] = tn(c_ref[...], ud[...])
    sums = scatter_sums(n, me, part, slots, send, recv)
    xg[0] = x_ref[...]
    cg[0] = c_ref[...]
    turn(xg, xt, 0)
    turn(cg, ct, 0)
    acc[...] = jnp.zeros_like(acc)
    second[0][...] = jnp.zeros_like(second[0])
    third[0][...] = jnp.zeros_like(third[0])
    crossing = cross_sums(n, me, part, slots, pair, send, recv, sums)
    rows = gather_sums(n, me, pair, lowf, send, recv, crossing)
    cs = {}
    for level in range(levels):
        xs[level].wait()
        cs[level] = to_partner(c_ref, cg.at[level + 1], 1, level)
        turn(xg, xt, level + 1)
    halves_to_twin(xg, x_p)
    for copy in rows:
        copy.wait()
    to_twin(lowf, lowf_p)
    for load in loads:
        load.wait()

    def add_slot(kind, slot, weights, hidden):
        def add(step, carry):
            cols = pl.ds(pl.multiple_of(step * block, block), block)
            term = nt(weights[slot, :, cols], hidden[:, cols])
            for b in range(per_panel):
                here = (tables[1 - kind][slot, base + step] == b).astype(F32)
                acc[slot, kind, b] += term * here
            return carry

        lax.fori_loop(0, steps, add, 0)

    def forward(step, carry):
        cols = pl.ds(pl.multiple_of(step * block, block), block)
        values = nt(lowf[0], vu[cols, :])
        for slot in range(slot_count):
            values = values + nn(xt[slot, tables[0][slot, base + step]], wu[slot, :, cols])
        cdf = 0.5 * (1.0 + lax.erf(values * root_half))
        slope[:, cols] = cdf + values * jnp.exp(-0.5 * values * values) * inv_root_tau
        hidden = (values * cdf).astype(BF16)
        act[:, cols] = hidden
        second[0][0] += nn(hidden, vd[cols, :])
        return carry

    def backward(step, carry):
        cols = pl.ds(pl.multiple_of(step * block, block), block)
        values = nt(lowf[1], vd[cols, :])
        for slot in range(slot_count):
            values = values + nn(ct[slot, tables[1][slot, base + step]], wd[slot, :, cols])
        hidden = (values * slope[:, cols]).astype(BF16)
        pre[:, cols] = hidden
        third[0][0] += nn(hidden, vu[cols, :])
        return carry

    def hand_on(kind, weights, hidden):
        copies = []
        for level in order:
            add_slot(kind, level + 1, weights, hidden)
            for b in range(per_panel):
                at = slice(b * block, (b + 1) * block)
                away[level, kind, at, :] = acc[level + 1, kind, b].astype(BF16)
            copies.append(to_partner(away.at[level, kind], home.at[level, kind], 2 + kind, level))
        add_slot(kind, 0, weights, hidden)
        for b in range(per_panel):
            own[kind, b * block : (b + 1) * block, :] = acc[0, kind, b]
        return copies

    lax.fori_loop(0, steps, forward, 0)
    part_a, slots_a, pair_a, send_a, recv_a = second
    sums_a = scatter_sums(n, me, part_a, slots_a, send_a, recv_a)
    to_twin(act, act_p)
    partials = hand_on(0, wd, act)
    for level in cs:
        cs[level].wait()
        turn(cg, ct, level + 1)
    halves_to_twin(cg, c_p)
    crossing_a = cross_sums(n, me, part_a, slots_a, pair_a, send_a, recv_a, sums_a)
    lax.fori_loop(0, steps, backward, 0)
    part_b, slots_b, pair_b, send_b, recv_b = third
    sums_b = scatter_sums(n, me, part_b, slots_b, send_b, recv_b)
    to_twin(pre, pre_p)
    partials = partials + hand_on(1, wu, pre)
    rows_a = gather_sums(n, me, pair_a, low_a, send_a, recv_a, crossing_a)
    crossing_b = cross_sums(n, me, part_b, slots_b, pair_b, send_b, recv_b, sums_b)
    rows_b = gather_sums(n, me, pair_b, low_b, send_b, recv_b, crossing_b)
    for copy in rows_a:
        copy.wait()
    to_twin(low_a, lowa_p)
    for copy in rows_b:
        copy.wait()
    to_twin(low_b, lowb_p)
    for copy in partials + twins:
        copy.wait()


def layer(table_up, table_down, features, cotangent, u_up, u_down, w_up, w_down, v_up, v_down, n):
    slot_count, block, hidden = w_up.shape
    levels = slot_count - 1
    dim, tokens = features.shape
    rank = u_up.shape[1]
    per_panel = dim // block
    vmem = pl.BlockSpec(memory_space=pltpu.VMEM)
    far = pl.BlockSpec(memory_space=pl.ANY)
    b16 = lambda *s: jax.ShapeDtypeStruct(s, BF16)
    copies = 7 + 2 * per_panel
    return pl.pallas_call(
        functools.partial(layer_kernel, n, levels, block),
        out_shape=(
            b16(slot_count, dim, tokens),
            b16(slot_count, dim, tokens),
            b16(2, tokens, rank),
            b16(tokens, hidden),
            b16(tokens, hidden),
            jax.ShapeDtypeStruct((2, dim, tokens), F32),
            b16(levels, 2, dim, tokens),
            b16(1, tokens, rank),
            b16(1, tokens, rank),
            b16(tokens, hidden),
            b16(tokens, hidden),
            b16(slot_count, per_panel, block // 2, tokens),
            b16(slot_count, per_panel, block // 2, tokens),
            b16(dim, tokens),
            b16(dim, tokens),
            b16(2, tokens, rank),
            b16(1, tokens, rank),
            b16(1, tokens, rank),
        ),
        in_specs=[pl.BlockSpec(memory_space=pltpu.SMEM)] * 2 + [vmem] * 4 + [far] * 4,
        out_specs=(vmem,) * 18,
        scratch_shapes=[
            *sum_scratch(n, 2, tokens, rank),
            *sum_scratch(n, 1, tokens, rank),
            *sum_scratch(n, 1, tokens, rank),
            pltpu.VMEM(w_up.shape, BF16),
            pltpu.VMEM(w_down.shape, BF16),
            pltpu.VMEM(v_up.shape, BF16),
            pltpu.VMEM(v_down.shape, BF16),
            pltpu.VMEM((slot_count, per_panel, tokens, block), BF16),
            pltpu.VMEM((slot_count, per_panel, tokens, block), BF16),
            pltpu.VMEM((tokens, hidden), F32),
            pltpu.VMEM((slot_count, 2, per_panel, block, tokens), F32),
            pltpu.VMEM((levels, 2, dim, tokens), BF16),
            pltpu.SemaphoreType.DMA((4,)),
            pltpu.SemaphoreType.DMA((4, levels)),
            pltpu.SemaphoreType.DMA((4, levels)),
            pltpu.SemaphoreType.DMA((copies,)),
            pltpu.SemaphoreType.DMA((copies,)),
        ],
        compiler_params=pltpu.CompilerParams(
            collective_id=0, has_side_effects=True, vmem_limit_bytes=VMEM_BYTES
        ),
    )(table_up, table_down, features, cotangent, u_up, u_down, w_up, w_down, v_up, v_down)


def final_kernel(
    slot_count,
    block,
    table_up,
    table_down,
    xg,
    cg,
    x_p,
    c_p,
    xown_p,
    cown_p,
    lowf,
    low_a,
    low_b,
    lowf_p,
    lowa_p,
    lowb_p,
    own,
    home,
    uu,
    ud,
    act,
    pre,
    act_p,
    pre_p,
    out,
    gfeat,
    gwu,
    gwd,
    guu,
    gvu,
    gud,
    gvd,
):
    step = pl.program_id(0)
    half = lax.axis_index("dp")
    base = lax.axis_index("tensor") * pl.num_programs(0)
    rows = block // 2
    width = lowf.shape[2] // 2
    cols = pl.ds(pl.multiple_of(half * width, width), width)
    for table, mine, twin, hid, hid_p, grad in (
        (table_up, xg, x_p, pre, pre_p, gwu),
        (table_down, cg, c_p, act, act_p, gwd),
    ):
        ours, theirs = [], []
        for slot in range(slot_count):
            b = table[slot, base + step]
            at = pl.ds(pl.multiple_of(b * block + half * rows, rows), rows)
            ours.append(mine[slot, at, :])
            theirs.append(twin[slot, b])
        total = nn(jnp.concatenate(ours), hid[...]) + nn(jnp.concatenate(theirs), hid_p[...])
        grad[...] = total.reshape(grad.shape)
    gvu[...] = tn(pre[...], lowf[0, :, cols]) + tn(pre_p[...], lowf_p[0, :, cols])
    gvd[...] = tn(act[...], lowf[1, :, cols]) + tn(act_p[...], lowf_p[1, :, cols])

    @pl.when(step == 0)
    def _():
        for kind, u, low, result in ((0, ud, low_a, out), (1, uu, low_b, gfeat)):
            total = own[kind] + nt(u[...], low[0])
            for level in range(slot_count - 1):
                total = total + home[level, kind].astype(F32)
            result[...] = total.astype(BF16)
        guu[...] = nn(xg[0], low_b[0, :, cols]) + nn(xown_p[...], lowb_p[0, :, cols])
        gud[...] = nn(cg[0], low_a[0, :, cols]) + nn(cown_p[...], lowa_p[0, :, cols])


def finish(table_up, table_down, xg, cg, x_p, c_p, xown_p, cown_p, lowf, low_a, low_b, lowf_p, lowa_p, lowb_p, own, home, u_up, u_down,
           act, pre, act_p, pre_p, block):
    slot_count, dim, tokens = xg.shape
    hidden = act.shape[1]
    rank = lowf.shape[2]
    full = lambda a: pl.BlockSpec(a.shape, lambda c, *_: (0,) * a.ndim)
    hid = pl.BlockSpec((tokens, block), lambda c, *_: (0, c))
    gw = pl.BlockSpec((slot_count, block // 2, block), lambda c, *_: (0, 0, c))
    gv = pl.BlockSpec((block, rank // 2), lambda c, *_: (c, 0))
    once = lambda *shape: pl.BlockSpec(shape, lambda c, *_: (0,) * len(shape))
    fixed = (xg, cg, x_p, c_p, xown_p, cown_p, lowf, low_a, low_b, lowf_p, lowa_p, lowb_p, own, home, u_up, u_down)
    return pl.pallas_call(
        functools.partial(final_kernel, slot_count, block),
        out_shape=(
            jax.ShapeDtypeStruct((dim, tokens), BF16),
            jax.ShapeDtypeStruct((dim, tokens), BF16),
            jax.ShapeDtypeStruct((slot_count, block // 2, hidden), F32),
            jax.ShapeDtypeStruct((slot_count, block // 2, hidden), F32),
            jax.ShapeDtypeStruct((dim, rank // 2), F32),
            jax.ShapeDtypeStruct((hidden, rank // 2), F32),
            jax.ShapeDtypeStruct((dim, rank // 2), F32),
            jax.ShapeDtypeStruct((hidden, rank // 2), F32),
        ),
        grid_spec=pltpu.PrefetchScalarGridSpec(
            num_scalar_prefetch=2,
            grid=(hidden // block,),
            in_specs=[full(a) for a in fixed] + [hid] * 4,
            out_specs=(
                once(dim, tokens),
                once(dim, tokens),
                gw,
                gw,
                once(dim, rank // 2),
                gv,
                once(dim, rank // 2),
                gv,
            ),
        ),
        compiler_params=pltpu.CompilerParams(vmem_limit_bytes=VMEM_BYTES),
    )(table_up, table_down, *fixed, act, pre, act_p, pre_p)


def one_panel_each(
    features, table_up, table_down, w_up, u_up, v_up, w_down, u_down, v_down, cotangent
):
    slot_count, block, hidden = w_up.shape
    levels = slot_count - 1
    n = lax.axis_size("tensor")
    (xg, cg, lowf, act, pre, own, home, low_a, low_b, act_p, pre_p, x_p, c_p, xown_p, cown_p, lowf_p,
     lowa_p, lowb_p) = layer(
        table_up, table_down, features, cotangent, u_up, u_down, w_up, w_down, v_up, v_down, n
    )
    return finish(table_up, table_down, xg, cg, x_p, c_p, xown_p, cown_p, lowf, low_a, low_b, lowf_p, lowa_p, lowb_p,
                  own, home, u_up, u_down, act, pre, act_p, pre_p, block)


def solve(*args):
    slot_count = args[3].shape[0]
    fits = (
        slot_count > 1
        and lax.axis_size("tensor") == 1 << slot_count - 1
        and lax.axis_size("dp") == 2
        and args[3].shape[2] % args[3].shape[1] == 0
    )
    return one_panel_each(*args) if fits else on_device(*args)


def solution(mesh):
    return jax.shard_map(
        solve,
        mesh=mesh,
        in_specs=(
            P("tensor", ("groups", "dp")),
            P(),
            P(),
            P(None, None, "tensor"),
            P("tensor", None),
            P("tensor", None),
            P(None, None, "tensor"),
            P("tensor", None),
            P("tensor", None),
            P("tensor", ("groups", "dp")),
        ),
        out_specs=(
            P("tensor", ("groups", "dp")),
            P("tensor", ("groups", "dp")),
            P("groups", "dp", "tensor"),
            P("groups", "dp", "tensor"),
            P(("groups", "tensor"), "dp"),
            P(("groups", "tensor"), "dp"),
            P(("groups", "tensor"), "dp"),
            P(("groups", "tensor"), "dp"),
        ),
        check_vma=False,
    )
```

```python
import functools
import math

import jax
import jax.numpy as jnp
from jax import lax
from jax.experimental import pallas as pl
from jax.experimental.pallas import tpu as pltpu
from jax.sharding import PartitionSpec as P

root_half = 1.0 / math.sqrt(2.0)
inv_root_tau = 1.0 / math.sqrt(2.0 * math.pi)


def from_partner(array, axis, distance):
    return lax.ppermute(array, axis, [(i, i ^ 1 << distance) for i in range(lax.axis_size(axis))])


def gelu_value(values):
    return 0.5 * values * (1.0 + lax.erf(values * root_half))


def gelu_slope(values):
    return (
        0.5 * (1.0 + lax.erf(values * root_half))
        + values * jnp.exp(-0.5 * values * values) * inv_root_tau
    )


def panel_trade(values, bit_index):
    return from_partner(values, "tensor", bit_index)


def partial_trade(values, bit_index):
    return from_partner(values, "tensor", bit_index)


def block_ids(device, geometry):
    block_rows, hidden, column_width, block_count = (
        geometry[3],
        geometry[4],
        geometry[5],
        geometry[6],
    )
    starts = device * hidden + jnp.arange(block_count, dtype=jnp.int32) * column_width
    return starts // block_rows


def lookup(selector, slot_index, device, geometry):
    return jnp.take(selector[slot_index], block_ids(device, geometry), axis=0)


def pick_blocks(panel_rows, chosen, block_rows):
    stacked = panel_rows.reshape(panel_rows.shape[0] // block_rows, block_rows, panel_rows.shape[1])
    return jnp.take(stacked, chosen, axis=0)


def place_blocks(portion, chosen, block_rows, panel_size):
    per_panel = panel_size // block_rows
    onehot = (chosen[:, None] == jnp.arange(per_panel, dtype=jnp.int32)[None, :]).astype(
        jnp.float32
    )
    placed = jnp.einsum("bn,brt->nrt", onehot, portion, precision=lax.Precision.HIGHEST)
    return placed.reshape(panel_size, portion.shape[2])


def group_gather(portion, axis_dim, group_bits, device):
    for bit_index in range(group_bits):
        partner_rows = panel_trade(portion, bit_index)
        is_upper = device >> bit_index & 1 == 1
        portion = jnp.where(
            is_upper,
            jnp.concatenate([partner_rows, portion], axis=axis_dim),
            jnp.concatenate([portion, partner_rows], axis=axis_dim),
        )
    return portion


def fetch_blocks(shard_rows, selector, geometry):
    device, group_bits, levels, block_rows = (geometry[0], geometry[1], geometry[2], geometry[3])
    own_panel = group_gather(shard_rows, 0, group_bits, device)
    selected = [pick_blocks(own_panel, lookup(selector, 0, device, geometry), block_rows)]
    for level_index in range(levels):
        bit_index = group_bits + level_index
        partner = device ^ 1 << bit_index
        wanted = pick_blocks(
            own_panel, lookup(selector, level_index + 1, partner, geometry), block_rows
        )
        selected.append(panel_trade(wanted, bit_index))
    return jnp.stack(selected)


def reduce_partials(contrib, selector, geometry):
    device, group_bits, levels, block_rows, panel_size = (
        geometry[0],
        geometry[1],
        geometry[2],
        geometry[3],
        geometry[7],
    )
    summed = place_blocks(contrib[0], lookup(selector, 0, device, geometry), block_rows, panel_size)
    for level_index in range(levels):
        bit_index = group_bits + level_index
        partner = device ^ 1 << bit_index
        arrived = partial_trade(contrib[level_index + 1], bit_index)
        summed = summed + place_blocks(
            arrived, lookup(selector, level_index + 1, partner, geometry), block_rows, panel_size
        )
    for bit_index in reversed(range(group_bits)):
        half_rows = summed.shape[0] // 2
        is_upper = device >> bit_index & 1 == 1
        kept_rows = jnp.where(is_upper, summed[half_rows:], summed[:half_rows])
        sent_rows = jnp.where(is_upper, summed[:half_rows], summed[half_rows:])
        summed = kept_rows + partial_trade(sent_rows, bit_index)
    return summed


def on_device(features, table_up, table_down, w_up, u_up, v_up, w_down, u_down, v_down, cotangent):
    device = lax.axis_index("tensor")
    slot_count, block_rows, hidden = w_up.shape
    levels = slot_count - 1
    group_bits = lax.axis_size("tensor").bit_length() - 1 - levels
    column_width = min(block_rows, hidden)
    block_count = hidden // column_width
    tokens_here = features.shape[1]
    panel_size = features.shape[0] * (1 << group_bits)
    geometry = (
        device,
        group_bits,
        levels,
        block_rows,
        hidden,
        column_width,
        block_count,
        panel_size,
    )
    up_blocks = w_up.reshape(slot_count, block_rows, block_count, column_width)
    down_blocks = w_down.reshape(slot_count, block_rows, block_count, column_width)
    a_up = lax.psum(jnp.dot(u_up.T, features, preferred_element_type=jnp.float32), "tensor")
    a_up_b = a_up.astype(jnp.bfloat16)
    picked_features = fetch_blocks(features, table_up, geometry)
    preact = jnp.einsum(
        "srbw,sbrt->bwt", up_blocks, picked_features, preferred_element_type=jnp.float32
    ).reshape(hidden, tokens_here)
    preact = preact + jnp.dot(v_up, a_up_b, preferred_element_type=jnp.float32)
    activation = gelu_value(preact).astype(jnp.bfloat16)
    a_down = lax.psum(jnp.dot(v_down.T, activation, preferred_element_type=jnp.float32), "tensor")
    a_down_b = a_down.astype(jnp.bfloat16)
    act_blocks = activation.reshape(block_count, column_width, tokens_here)
    partial_out = jnp.einsum(
        "srbw,bwt->sbrt", down_blocks, act_blocks, preferred_element_type=jnp.float32
    )
    output = (
        reduce_partials(partial_out, table_down, geometry)
        + jnp.dot(u_down, a_down_b, preferred_element_type=jnp.float32)
    ).astype(jnp.bfloat16)
    b_down = lax.psum(jnp.dot(u_down.T, cotangent, preferred_element_type=jnp.float32), "tensor")
    b_down_b = b_down.astype(jnp.bfloat16)
    picked_cotangent = fetch_blocks(cotangent, table_down, geometry)
    grad_act = jnp.einsum(
        "srbw,sbrt->bwt", down_blocks, picked_cotangent, preferred_element_type=jnp.float32
    ).reshape(hidden, tokens_here)
    grad_act = grad_act + jnp.dot(v_down, b_down_b, preferred_element_type=jnp.float32)
    grad_pre = (grad_act * gelu_slope(preact)).astype(jnp.bfloat16)
    grad_w_down = jnp.einsum(
        "sbrt,bwt->srbw", picked_cotangent, act_blocks, preferred_element_type=jnp.float32
    ).reshape(slot_count, block_rows, hidden)
    grad_u_down = jnp.dot(cotangent, a_down_b.T, preferred_element_type=jnp.float32)
    grad_v_down = jnp.dot(activation, b_down_b.T, preferred_element_type=jnp.float32)
    grad_w_down, grad_u_down, grad_v_down = (
        lax.psum_scatter(grad_w_down, "dp", scatter_dimension=1, tiled=True),
        lax.psum_scatter(grad_u_down, "dp", scatter_dimension=1, tiled=True),
        lax.psum_scatter(grad_v_down, "dp", scatter_dimension=1, tiled=True),
    )
    b_up = lax.psum(jnp.dot(v_up.T, grad_pre, preferred_element_type=jnp.float32), "tensor")
    b_up_b = b_up.astype(jnp.bfloat16)
    pre_blocks = grad_pre.reshape(block_count, column_width, tokens_here)
    partial_back = jnp.einsum(
        "srbw,bwt->sbrt", up_blocks, pre_blocks, preferred_element_type=jnp.float32
    )
    grad_features = (
        reduce_partials(partial_back, table_up, geometry)
        + jnp.dot(u_up, b_up_b, preferred_element_type=jnp.float32)
    ).astype(jnp.bfloat16)
    grad_w_up = jnp.einsum(
        "sbrt,bwt->srbw", picked_features, pre_blocks, preferred_element_type=jnp.float32
    ).reshape(slot_count, block_rows, hidden)
    grad_u_up = jnp.dot(features, b_up_b.T, preferred_element_type=jnp.float32)
    grad_v_up = jnp.dot(grad_pre, a_up_b.T, preferred_element_type=jnp.float32)
    grad_w_up, grad_u_up, grad_v_up = (
        lax.psum_scatter(grad_w_up, "dp", scatter_dimension=1, tiled=True),
        lax.psum_scatter(grad_u_up, "dp", scatter_dimension=1, tiled=True),
        lax.psum_scatter(grad_v_up, "dp", scatter_dimension=1, tiled=True),
    )
    return (
        output,
        grad_features,
        grad_w_up,
        grad_w_down,
        grad_u_up,
        grad_v_up,
        grad_u_down,
        grad_v_down,
    )


F32, BF16 = jnp.float32, jnp.bfloat16
VMEM_BYTES = 56 * 2**20


def nn(a, b):
    return lax.dot_general(a, b, (((1,), (0,)), ((), ())), preferred_element_type=F32)


def nt(a, b):
    return lax.dot_general(a, b, (((1,), (1,)), ((), ())), preferred_element_type=F32)


def tn(a, b):
    return lax.dot_general(a, b, (((0,), (0,)), ((), ())), preferred_element_type=F32)


def flip(me, offset):
    peer = me
    for k in range(offset.bit_length()):
        if offset >> k & 1:
            peer = peer + (1 << k) * (1 - 2 * ((me // (1 << k)) % 2))
    return peer


def remote(src, dst, send_sem, recv_sem, device_id):
    copy = pltpu.make_async_remote_copy(
        src_ref=src,
        dst_ref=dst,
        send_sem=send_sem,
        recv_sem=recv_sem,
        device_id=device_id,
        device_id_type=pl.DeviceIdType.MESH,
    )
    copy.start()
    return copy


def meet(n, me, half):
    barrier = pltpu.get_barrier_semaphore()
    for offset in range(1, n):
        pl.semaphore_signal(
            barrier,
            inc=1,
            device_id={"tensor": flip(me, offset)},
            device_id_type=pl.DeviceIdType.MESH,
        )
    count = n - 1
    if half is not None:
        pl.semaphore_signal(
            barrier, inc=1, device_id={"dp": 1 - half}, device_id_type=pl.DeviceIdType.MESH
        )
        count += 1
    pl.semaphore_wait(barrier, count)


def scatter_sums(n, me, part, slots, send, recv):
    group = n // 2
    rows = part.shape[1] // group
    copies = []
    for offset in range(1, group):
        peer = flip(me, offset)
        at = pl.ds(pl.multiple_of(peer % group * rows, rows), rows)
        copies.append(
            remote(
                part.at[:, at, :],
                slots.at[offset],
                send.at[0, offset],
                recv.at[0, offset],
                {"tensor": peer},
            )
        )
    return copies


def cross_sums(n, me, part, slots, pair, send, recv, copies):
    group = n // 2
    rows = part.shape[1] // group
    mine = pl.ds(pl.multiple_of(me % group * rows, rows), rows)
    for copy in copies:
        copy.wait()
    summed = part[:, mine, :]
    for offset in range(1, group):
        summed = summed + slots[offset]
    pair[0] = summed
    return remote(
        pair.at[0], pair.at[1], send.at[0, 0], recv.at[0, 0], {"tensor": flip(me, group)}
    )


def gather_sums(n, me, pair, total, send, recv, copy):
    group = n // 2
    rows = pair.shape[2]
    mine = pl.ds(pl.multiple_of(me % group * rows, rows), rows)
    copy.wait()
    total[:, mine, :] = (pair[0] + pair[1]).astype(BF16)
    return [
        remote(
            total.at[:, mine, :],
            total.at[:, mine, :],
            send.at[1, offset],
            recv.at[1, offset],
            {"tensor": flip(me, offset)},
        )
        for offset in range(1, group)
    ]


def sum_scratch(n, lead, tokens, rank):
    group = n // 2
    return [
        pltpu.VMEM((lead, tokens, rank), F32),
        pltpu.VMEM((group, lead, tokens // group, rank), F32),
        pltpu.VMEM((2, lead, tokens // group, rank), F32),
        pltpu.SemaphoreType.DMA((2, group)),
        pltpu.SemaphoreType.DMA((2, group)),
    ]


def layer_kernel(n, levels, block, table_up, table_down, x_ref, c_ref, uu, ud, wu_any, wd_any, vu_any, vd_any, *refs):
    (xg, cg, lowf, act, pre, own, home, low_a, low_b, act_p, pre_p, x_p, c_p) = refs[:13]
    (xown_p, cown_p, lowf_p, lowa_p, lowb_p) = refs[13:18]
    first, second, third = refs[18:23], refs[23:28], refs[28:33]
    (wu, wd, vu, vd, xt, ct, slope, acc, away, lsem, psend, precv, dsend, drecv) = refs[33:]
    me = lax.axis_index("tensor")
    half = lax.axis_index("dp")
    twin = {"dp": 1 - half}
    slot_count = levels + 1
    per_panel = x_ref.shape[0] // block
    steps = act.shape[1] // block
    tables = (table_up, table_down)
    base = me * steps
    loads = []
    for k, (src, dst) in enumerate(((wu_any, wu), (vu_any, vu), (wd_any, wd), (vd_any, vd))):
        loads.append(pltpu.make_async_copy(src, dst, lsem.at[k]))
        loads[-1].start()
    meet(n, me, half)

    def to_partner(src, dst, kind, level):
        return remote(
            src,
            dst,
            psend.at[kind, level],
            precv.at[kind, level],
            {"tensor": flip(me, 1 << level)},
        )

    twins = []

    def to_twin(src, dst):
        k = len(twins)
        twins.append(remote(src, dst, dsend.at[k], drecv.at[k], twin))

    def halves_to_twin(rows_ref, dst):
        rows = block // 2
        for b in range(per_panel):
            at = pl.ds(pl.multiple_of(b * block + (1 - half) * rows, rows), rows)
            to_twin(rows_ref.at[:, at, :], dst.at[:, b])

    def turn(panels, turned, slot):
        for b in range(per_panel):
            turned[slot, b] = panels[slot, b * block : (b + 1) * block, :].T

    order = tuple(reversed(range(levels)))
    xs = {level: to_partner(x_ref, xg.at[level + 1], 0, level) for level in order}
    to_twin(x_ref, xown_p)
    to_twin(c_ref, cown_p)
    part, slots, pair, send, recv = first
    part[0] = tn(x_ref[...], uu[...])
    part[1] = tn(c_ref[...], ud[...])
    sums = scatter_sums(n, me, part, slots, send, recv)
    xg[0] = x_ref[...]
    cg[0] = c_ref[...]
    turn(xg, xt, 0)
    turn(cg, ct, 0)
    acc[...] = jnp.zeros_like(acc)
    second[0][...] = jnp.zeros_like(second[0])
    third[0][...] = jnp.zeros_like(third[0])
    crossing = cross_sums(n, me, part, slots, pair, send, recv, sums)
    cs = {level: to_partner(c_ref, cg.at[level + 1], 1, level) for level in order}
    rows = gather_sums(n, me, pair, lowf, send, recv, crossing)
    for level in range(levels):
        xs[level].wait()
        turn(xg, xt, level + 1)
    halves_to_twin(xg, x_p)
    for copy in rows:
        copy.wait()
    to_twin(lowf, lowf_p)
    for load in loads:
        load.wait()

    def add_slot(kind, slot, weights, hidden):
        def add(step, carry):
            cols = pl.ds(pl.multiple_of(step * block, block), block)
            term = nt(weights[slot, :, cols], hidden[:, cols])
            for b in range(per_panel):
                here = (tables[1 - kind][slot, base + step] == b).astype(F32)
                acc[slot, kind, b] += term * here
            return carry

        lax.fori_loop(0, steps, add, 0)

    def forward(step, carry):
        cols = pl.ds(pl.multiple_of(step * block, block), block)
        values = nt(lowf[0], vu[cols, :])
        for slot in range(slot_count):
            values = values + nn(xt[slot, tables[0][slot, base + step]], wu[slot, :, cols])
        cdf = 0.5 * (1.0 + lax.erf(values * root_half))
        slope[:, cols] = cdf + values * jnp.exp(-0.5 * values * values) * inv_root_tau
        hidden = (values * cdf).astype(BF16)
        act[:, cols] = hidden
        second[0][0] += nn(hidden, vd[cols, :])
        return carry

    def backward(step, carry):
        cols = pl.ds(pl.multiple_of(step * block, block), block)
        values = nt(lowf[1], vd[cols, :])
        for slot in range(slot_count):
            values = values + nn(ct[slot, tables[1][slot, base + step]], wd[slot, :, cols])
        hidden = (values * slope[:, cols]).astype(BF16)
        pre[:, cols] = hidden
        third[0][0] += nn(hidden, vu[cols, :])
        return carry

    def hand_on(kind, weights, hidden):
        copies = []
        for level in order:
            add_slot(kind, level + 1, weights, hidden)
            for b in range(per_panel):
                at = slice(b * block, (b + 1) * block)
                away[level, kind, at, :] = acc[level + 1, kind, b].astype(BF16)
            copies.append(to_partner(away.at[level, kind], home.at[level, kind], 2 + kind, level))
        add_slot(kind, 0, weights, hidden)
        for b in range(per_panel):
            own[kind, b * block : (b + 1) * block, :] = acc[0, kind, b]
        return copies

    lax.fori_loop(0, steps, forward, 0)
    part_a, slots_a, pair_a, send_a, recv_a = second
    sums_a = scatter_sums(n, me, part_a, slots_a, send_a, recv_a)
    to_twin(act, act_p)
    partials = hand_on(0, wd, act)
    for level in range(levels):
        cs[level].wait()
        turn(cg, ct, level + 1)
    halves_to_twin(cg, c_p)
    crossing_a = cross_sums(n, me, part_a, slots_a, pair_a, send_a, recv_a, sums_a)
    lax.fori_loop(0, steps, backward, 0)
    part_b, slots_b, pair_b, send_b, recv_b = third
    sums_b = scatter_sums(n, me, part_b, slots_b, send_b, recv_b)
    to_twin(pre, pre_p)
    partials = partials + hand_on(1, wu, pre)
    rows_a = gather_sums(n, me, pair_a, low_a, send_a, recv_a, crossing_a)
    crossing_b = cross_sums(n, me, part_b, slots_b, pair_b, send_b, recv_b, sums_b)
    rows_b = gather_sums(n, me, pair_b, low_b, send_b, recv_b, crossing_b)
    for copy in rows_a:
        copy.wait()
    to_twin(low_a, lowa_p)
    for copy in rows_b:
        copy.wait()
    to_twin(low_b, lowb_p)
    for copy in partials + twins:
        copy.wait()


def layer(table_up, table_down, features, cotangent, u_up, u_down, w_up, w_down, v_up, v_down, n):
    slot_count, block, hidden = w_up.shape
    levels = slot_count - 1
    dim, tokens = features.shape
    rank = u_up.shape[1]
    per_panel = dim // block
    vmem = pl.BlockSpec(memory_space=pltpu.VMEM)
    far = pl.BlockSpec(memory_space=pl.ANY)
    b16 = lambda *s: jax.ShapeDtypeStruct(s, BF16)
    copies = 7 + 2 * per_panel
    return pl.pallas_call(
        functools.partial(layer_kernel, n, levels, block),
        out_shape=(
            b16(slot_count, dim, tokens),
            b16(slot_count, dim, tokens),
            b16(2, tokens, rank),
            b16(tokens, hidden),
            b16(tokens, hidden),
            jax.ShapeDtypeStruct((2, dim, tokens), F32),
            b16(levels, 2, dim, tokens),
            b16(1, tokens, rank),
            b16(1, tokens, rank),
            b16(tokens, hidden),
            b16(tokens, hidden),
            b16(slot_count, per_panel, block // 2, tokens),
            b16(slot_count, per_panel, block // 2, tokens),
            b16(dim, tokens),
            b16(dim, tokens),
            b16(2, tokens, rank),
            b16(1, tokens, rank),
            b16(1, tokens, rank),
        ),
        in_specs=[pl.BlockSpec(memory_space=pltpu.SMEM)] * 2 + [vmem] * 4 + [far] * 4,
        out_specs=(vmem,) * 18,
        scratch_shapes=[
            *sum_scratch(n, 2, tokens, rank),
            *sum_scratch(n, 1, tokens, rank),
            *sum_scratch(n, 1, tokens, rank),
            pltpu.VMEM(w_up.shape, BF16),
            pltpu.VMEM(w_down.shape, BF16),
            pltpu.VMEM(v_up.shape, BF16),
            pltpu.VMEM(v_down.shape, BF16),
            pltpu.VMEM((slot_count, per_panel, tokens, block), BF16),
            pltpu.VMEM((slot_count, per_panel, tokens, block), BF16),
            pltpu.VMEM((tokens, hidden), F32),
            pltpu.VMEM((slot_count, 2, per_panel, block, tokens), F32),
            pltpu.VMEM((levels, 2, dim, tokens), BF16),
            pltpu.SemaphoreType.DMA((4,)),
            pltpu.SemaphoreType.DMA((4, levels)),
            pltpu.SemaphoreType.DMA((4, levels)),
            pltpu.SemaphoreType.DMA((copies,)),
            pltpu.SemaphoreType.DMA((copies,)),
        ],
        compiler_params=pltpu.CompilerParams(
            collective_id=0, has_side_effects=True, vmem_limit_bytes=VMEM_BYTES
        ),
    )(table_up, table_down, features, cotangent, u_up, u_down, w_up, w_down, v_up, v_down)


def final_kernel(
    slot_count,
    block,
    table_up,
    table_down,
    xg,
    cg,
    x_p,
    c_p,
    xown_p,
    cown_p,
    lowf,
    low_a,
    low_b,
    lowf_p,
    lowa_p,
    lowb_p,
    own,
    home,
    uu,
    ud,
    act,
    pre,
    act_p,
    pre_p,
    out,
    gfeat,
    gwu,
    gwd,
    guu,
    gvu,
    gud,
    gvd,
):
    step = pl.program_id(0)
    half = lax.axis_index("dp")
    base = lax.axis_index("tensor") * pl.num_programs(0)
    rows = block // 2
    width = lowf.shape[2] // 2
    cols = pl.ds(pl.multiple_of(half * width, width), width)
    for table, mine, twin, hid, hid_p, grad in (
        (table_up, xg, x_p, pre, pre_p, gwu),
        (table_down, cg, c_p, act, act_p, gwd),
    ):
        ours, theirs = [], []
        for slot in range(slot_count):
            b = table[slot, base + step]
            at = pl.ds(pl.multiple_of(b * block + half * rows, rows), rows)
            ours.append(mine[slot, at, :])
            theirs.append(twin[slot, b])
        total = nn(jnp.concatenate(ours), hid[...]) + nn(jnp.concatenate(theirs), hid_p[...])
        grad[...] = total.reshape(grad.shape)
    gvu[...] = tn(pre[...], lowf[0, :, cols]) + tn(pre_p[...], lowf_p[0, :, cols])
    gvd[...] = tn(act[...], lowf[1, :, cols]) + tn(act_p[...], lowf_p[1, :, cols])

    @pl.when(step == 0)
    def _():
        for kind, u, low, result in ((0, ud, low_a, out), (1, uu, low_b, gfeat)):
            total = own[kind] + nt(u[...], low[0])
            for level in range(slot_count - 1):
                total = total + home[level, kind].astype(F32)
            result[...] = total.astype(BF16)
        guu[...] = nn(xg[0], low_b[0, :, cols]) + nn(xown_p[...], lowb_p[0, :, cols])
        gud[...] = nn(cg[0], low_a[0, :, cols]) + nn(cown_p[...], lowa_p[0, :, cols])


def finish(table_up, table_down, xg, cg, x_p, c_p, xown_p, cown_p, lowf, low_a, low_b, lowf_p, lowa_p, lowb_p, own, home, u_up, u_down,
           act, pre, act_p, pre_p, block):
    slot_count, dim, tokens = xg.shape
    hidden = act.shape[1]
    rank = lowf.shape[2]
    full = lambda a: pl.BlockSpec(a.shape, lambda c, *_: (0,) * a.ndim)
    hid = pl.BlockSpec((tokens, block), lambda c, *_: (0, c))
    gw = pl.BlockSpec((slot_count, block // 2, block), lambda c, *_: (0, 0, c))
    gv = pl.BlockSpec((block, rank // 2), lambda c, *_: (c, 0))
    once = lambda *shape: pl.BlockSpec(shape, lambda c, *_: (0,) * len(shape))
    fixed = (xg, cg, x_p, c_p, xown_p, cown_p, lowf, low_a, low_b, lowf_p, lowa_p, lowb_p, own, home, u_up, u_down)
    return pl.pallas_call(
        functools.partial(final_kernel, slot_count, block),
        out_shape=(
            jax.ShapeDtypeStruct((dim, tokens), BF16),
            jax.ShapeDtypeStruct((dim, tokens), BF16),
            jax.ShapeDtypeStruct((slot_count, block // 2, hidden), F32),
            jax.ShapeDtypeStruct((slot_count, block // 2, hidden), F32),
            jax.ShapeDtypeStruct((dim, rank // 2), F32),
            jax.ShapeDtypeStruct((hidden, rank // 2), F32),
            jax.ShapeDtypeStruct((dim, rank // 2), F32),
            jax.ShapeDtypeStruct((hidden, rank // 2), F32),
        ),
        grid_spec=pltpu.PrefetchScalarGridSpec(
            num_scalar_prefetch=2,
            grid=(hidden // block,),
            in_specs=[full(a) for a in fixed] + [hid] * 4,
            out_specs=(
                once(dim, tokens),
                once(dim, tokens),
                gw,
                gw,
                once(dim, rank // 2),
                gv,
                once(dim, rank // 2),
                gv,
            ),
        ),
        compiler_params=pltpu.CompilerParams(vmem_limit_bytes=VMEM_BYTES),
    )(table_up, table_down, *fixed, act, pre, act_p, pre_p)


def one_panel_each(
    features, table_up, table_down, w_up, u_up, v_up, w_down, u_down, v_down, cotangent
):
    slot_count, block, hidden = w_up.shape
    levels = slot_count - 1
    n = lax.axis_size("tensor")
    (xg, cg, lowf, act, pre, own, home, low_a, low_b, act_p, pre_p, x_p, c_p, xown_p, cown_p, lowf_p,
     lowa_p, lowb_p) = layer(
        table_up, table_down, features, cotangent, u_up, u_down, w_up, w_down, v_up, v_down, n
    )
    return finish(table_up, table_down, xg, cg, x_p, c_p, xown_p, cown_p, lowf, low_a, low_b, lowf_p, lowa_p, lowb_p,
                  own, home, u_up, u_down, act, pre, act_p, pre_p, block)


def solve(*args):
    slot_count = args[3].shape[0]
    fits = (
        slot_count > 1
        and lax.axis_size("tensor") == 1 << slot_count - 1
        and lax.axis_size("dp") == 2
        and args[3].shape[2] % args[3].shape[1] == 0
    )
    return one_panel_each(*args) if fits else on_device(*args)


def solution(mesh):
    return jax.shard_map(
        solve,
        mesh=mesh,
        in_specs=(
            P("tensor", ("groups", "dp")),
            P(),
            P(),
            P(None, None, "tensor"),
            P("tensor", None),
            P("tensor", None),
            P(None, None, "tensor"),
            P("tensor", None),
            P("tensor", None),
            P("tensor", ("groups", "dp")),
        ),
        out_specs=(
            P("tensor", ("groups", "dp")),
            P("tensor", ("groups", "dp")),
            P("groups", "dp", "tensor"),
            P("groups", "dp", "tensor"),
            P(("groups", "tensor"), "dp"),
            P(("groups", "tensor"), "dp"),
            P(("groups", "tensor"), "dp"),
            P(("groups", "tensor"), "dp"),
        ),
        check_vma=False,
    )
```
